32 devices in a mesh: layer: 2 (over x), head: 16 (over z, y, core).
Axes of the slice: x: 2, y: 2, z: 4, core: 2. Of those that a mesh axis runs over, the one named last changes fastest.
Arguments:
- queries: bfloat16 [4, 48, 512, 128], P('layer', 'head'), may hold values from -4.5 to 4.5
- keys: bfloat16 [4, 48, 512, 128], P('layer', 'head'), may hold values from -4.5 to 4.5
- head_weight: float32 [4, 40], P('layer'), may hold values from -180 to 180
- slot_head: int32 [48], P('head'), may hold values from 0 to 40, as said below
- target: int32 [512, 512], P('head'), may hold values 0 or 1
Outputs:
- query_grad: bfloat16 [4, 48, 512, 128], P('layer', 'head')
- key_grad: bfloat16 [4, 48, 512, 128], P('layer', 'head')
- weight_grad: float32 [4, 48], P('layer', 'head')
The draws below stay inside these ranges and needn't reach their ends.
Inputs may be any that keep to these rules, and one draw needn't show every extreme that they name: `slot_head`: each head 0 to 39 is held by exactly one slot; every other slot holds 40.
All inputs are finite; a program needn't handle non-finite values. No bound on the sum of `target` on one device may be relied on, other than what follows from the above.
Results may differ from the reference program's by a relative error of at most 0.0051.
Values sent between devices are 32-bit elements; how exact they have to be, the bound alone decides.
No kernel may reach another device: no remote copies, remote signals or barrier semaphores. Data moves between devices by JAX's collectives and lax.ppermute only.
A program may use at most 64 MiB of HBM per device.

```python
import jax
import jax.numpy as jnp
from jax import lax

L = 512
HEADS = 40
DH = 128
LAYERS = 4
SLOTS = 48


def pair_draw(key):
    key_q, key_k = jax.random.split(jax.random.fold_in(key, 11), 2)
    shape = (LAYERS, SLOTS, L, DH)
    query = jnp.clip(jax.random.normal(key_q, shape, jnp.float32), -4.5, 4.5)
    keyarr = jnp.clip(jax.random.normal(key_k, shape, jnp.float32), -4.5, 4.5)
    return (query, keyarr)


def draw_queries(key, part):
    return pair_draw(key)[0].astype(jnp.bfloat16)


def draw_keys(key, part):
    return pair_draw(key)[1].astype(jnp.bfloat16)


def draw_slot_head(key, part):
    order = jax.random.permutation(jax.random.fold_in(key, 23), SLOTS)
    return jnp.minimum(order, HEADS).astype(jnp.int32)


def plant(values, stream_key, low, largest):
    dims = values.shape
    place = [jax.random.randint(jax.random.fold_in(stream_key, axis), (), 0, dims[axis]) for axis in range(len(dims))]
    values = values.at[tuple(place)].set(low)
    longest = dims.index(max(dims))
    place[longest] = (place[longest] + 1) % dims[longest]
    return values.at[tuple(place)].set(largest)


def shard_levels(own_key, extent, shards, low, top_value):
    loudness, own = 1.0, jax.random.fold_in(own_key, 6)
    for position, parts in shards:
        heights = jnp.exp(jax.random.uniform(jax.random.fold_in(own, position), (parts,), jnp.float32, low / len(shards), top_value / len(shards)))
        loudness = loudness * jnp.repeat(heights, extent[position] // parts).reshape([-1 if axis == position else 1 for axis in range(len(extent))])
    return loudness


def normal_values(own_key, extent, spread, most, shards=(), held_as=jnp.bfloat16):
    result = jax.random.normal(own_key, extent, jnp.float32) * spread
    if len(shards) > 0:
        result = shard_levels(own_key, extent, shards, -0.22, 0.18) * result
    return jnp.clip(result, min=-most, max=most).astype(held_as)


def setup_inputs(seed: int = 0) -> dict:
    arg_keys = jax.random.split(jax.random.key(seed), 6)
    return {
        "queries": draw_queries(jax.random.fold_in(arg_keys[5], 71), 0),
        "keys": draw_keys(jax.random.fold_in(arg_keys[5], 71), 0),
        "head_weight": normal_values(arg_keys[2], (LAYERS, HEADS), 30.0, 180.0, ((0, 2),), jnp.float32),
        "slot_head": draw_slot_head(jax.random.fold_in(arg_keys[5], 71), 0),
        "target": plant((jax.random.randint(arg_keys[4], (L, L), 0, 16) < 1).astype(jnp.int32), jax.random.fold_in(arg_keys[4], 1), 0, 1),
    }


def pair_maps(query, key):
    scale = DH ** -0.5
    scores = jnp.dot(query, key.T, preferred_element_type=jnp.float32) * scale
    highest = jnp.max(scores, axis=1, keepdims=True)
    expo = jnp.exp(scores - highest)
    probs = expo / jnp.sum(expo, axis=1, keepdims=True)
    sym = probs + probs.T
    rowsum = jnp.sum(sym, axis=1)
    total = jnp.sum(rowsum)
    feature = sym - rowsum[:, None] * rowsum[None, :] / total
    return probs, rowsum, total, feature


def pair_back(query, key, weight, error):
    scale = DH ** -0.5
    probs, rowsum, total, feature = pair_maps(query, key)
    wgrad = jnp.sum(error * feature)
    gmap = weight * error
    u_vec = jnp.sum(gmap * rowsum[None, :], axis=1)
    v_vec = jnp.sum(gmap * rowsum[:, None], axis=0)
    dsym = gmap - (u_vec[:, None] + v_vec[None, :]) / total + jnp.sum(rowsum * u_vec) / (total * total)
    dprobs = dsym + dsym.T
    dscores = probs * (dprobs - jnp.sum(probs * dprobs, axis=1, keepdims=True))
    dscores = dscores.astype(jnp.bfloat16)
    qgrad = (jnp.dot(dscores, key, preferred_element_type=jnp.float32) * scale).astype(jnp.bfloat16)
    kgrad = (jnp.dot(dscores.T, query, preferred_element_type=jnp.float32) * scale).astype(jnp.bfloat16)
    return qgrad, kgrad, wgrad


def reference(queries, keys, head_weight, slot_head, target):
    onehot = (slot_head[:, None] == jnp.arange(HEADS, dtype=jnp.int32)[None, :]).astype(jnp.float32)
    slot_weight = jnp.dot(head_weight, onehot.T, precision=lax.Precision.HIGHEST)
    flat_q = queries.reshape(LAYERS * SLOTS, L, DH)
    flat_k = keys.reshape(LAYERS * SLOTS, L, DH)
    flat_w = slot_weight.reshape(LAYERS * SLOTS)

    def add_pair(total, item):
        query, key, weight = item
        feature = pair_maps(query, key)[3]
        return total + weight * feature, None

    logit, _ = lax.scan(add_pair, jnp.zeros((L, L), jnp.float32), (flat_q, flat_k, flat_w))
    error = jax.nn.sigmoid(logit) - target.astype(jnp.float32)

    def back_pair(item):
        query, key, weight = item
        return pair_back(query, key, weight, error)

    qgrad, kgrad, wgrad = lax.map(back_pair, (flat_q, flat_k, flat_w))
    return (qgrad.reshape(LAYERS, SLOTS, L, DH), kgrad.reshape(LAYERS, SLOTS, L, DH), wgrad.reshape(LAYERS, SLOTS))
```

```python
import functools

import jax
import jax.numpy as jnp
from jax import lax
from jax.experimental import pallas as pl
from jax.experimental.pallas import tpu as pltpu
from jax.sharding import PartitionSpec as P

TILE = 128


def block_pairs(count):
    pairs = []
    for row in range(count):
        for col in range(count):
            gap = (col - row) % count
            if 2 * gap < count or (2 * gap == count and row < col):
                pairs.append((row, col))
    return pairs


def pad8(count):
    return -(-count // 8) * 8


def split3(value):
    first = value.astype(jnp.bfloat16).astype(jnp.float32)
    rest = value - first
    second = rest.astype(jnp.bfloat16).astype(jnp.float32)
    return first, second, rest - second


def pair_weight(hw_ref, head_ref, pair, slot_count, heads):
    layer, slot = pair // slot_count, pair % slot_count
    held = head_ref[slot]
    return jnp.where(held < heads, hw_ref[layer, jnp.minimum(held, heads - 1)], 0.0)


class Plan:
    def __init__(self, layers, heads, length):
        self.blocks = length // TILE
        self.pairs = block_pairs(self.blocks)
        self.layers, self.heads = layers, heads
        self.fast = (
            heads % 4 == 0
            and heads // 4 == self.blocks
            and self.blocks & (self.blocks - 1) == 0
            and layers & (layers - 1) == 0
            and (TILE // (4 * layers)) % 8 == 0
        )
        self.halves = 2 if self.fast else 1
        self.positions = 2 * layers if self.fast else 1
        self.rows = TILE // (self.halves * self.positions)

    def offset(self, half, position):
        if not self.fast:
            return 0
        head = lax.axis_index("head")
        core = (head % 2) ^ half
        y_at = ((head // 2) % 2) ^ (position % 2)
        layer = lax.axis_index("layer") ^ (position // 2)
        return ((2 * y_at + core) * self.layers + layer) * self.rows


def forward_kernel(plan, slot_count, heads, count, hw_ref, head_ref, q_ref, k_ref, *rest):
    outs, probs_ref, rsum_ref = rest[: plan.halves], rest[plan.halves], rest[plan.halves + 1]
    acc, scaled = rest[plan.halves + 2 :]
    pair = pl.program_id(0)
    length = q_ref.shape[1]
    scale = q_ref.shape[2] ** (-0.5)
    total = 2.0 * length
    weight = pair_weight(hw_ref, head_ref, pair, slot_count, heads)

    @pl.when(pair == 0)
    def _():
        acc[...] = jnp.zeros_like(acc)
        scaled[...] = jnp.zeros_like(scaled)
        rsum_ref[...] = jnp.zeros_like(rsum_ref)

    colsum = jnp.ones((1, length), jnp.float32)
    key = k_ref[0]
    for part in range(length // TILE):
        rows = slice(part * TILE, (part + 1) * TILE)
        scores = lax.dot_general(
            q_ref[0, rows, :], key, (((1,), (1,)), ((), ())), preferred_element_type=jnp.float32
        )
        highest = jnp.max(scores, axis=1, keepdims=True)
        expo = jnp.exp((scores - highest) * scale)
        probs = expo * (1.0 / jnp.sum(expo, axis=1, keepdims=True))
        probs_ref[0, rows, :] = probs.astype(probs_ref.dtype)
        acc[rows, :] += weight * probs
        colsum = colsum + jnp.sum(probs, axis=0, keepdims=True)
    rsum_ref[pl.ds(pair, 1), :] = colsum
    scaled[pl.ds(pair, 1), :] = colsum * (-weight / total)

    @pl.when(pair == count - 1)
    def _():
        left = split3(scaled[...])
        right = split3(rsum_ref[...])
        order = ((0, 0), (0, 1), (1, 0), (1, 1), (0, 2), (2, 0))
        lefts = jnp.concatenate([left[a] for a, _ in order], axis=0).astype(jnp.bfloat16)
        rights = jnp.concatenate([right[b] for _, b in order], axis=0).astype(jnp.bfloat16)
        for at, (row, col) in enumerate(plan.pairs):
            rs, cs = slice(row * TILE, (row + 1) * TILE), slice(col * TILE, (col + 1) * TILE)
            both = acc[rs, cs] + acc[cs, rs].T
            both = both + lax.dot_general(
                lefts[:, rs], rights[:, cs], (((0,), (0,)), ((), ())), preferred_element_type=jnp.float32
            )
            acc[rs, cs] = both
        for half in range(plan.halves):
            for position in range(plan.positions):
                off = pl.multiple_of(plan.offset(half, position), 8)
                for at, (row, col) in enumerate(plan.pairs):
                    outs[half][position, at * plan.rows : (at + 1) * plan.rows, :] = acc[
                        pl.ds(row * TILE + off, plan.rows), col * TILE : (col + 1) * TILE
                    ]


def backward_kernel(plan, slot_count, heads, count, hw_ref, head_ref, q_ref, k_ref, probs_ref, rsum_ref, *rest):
    packed = rest[: plan.halves]
    qg_ref, kg_ref, wg_ref, fmat, zmat, dmat = rest[plan.halves :]
    pair = pl.program_id(0)
    length = q_ref.shape[1]
    scale = q_ref.shape[2] ** (-0.5)
    total = 2.0 * length
    weight = pair_weight(hw_ref, head_ref, pair, slot_count, heads)

    @pl.when(pair == 0)
    def _():
        for half in range(plan.halves):
            for position in range(plan.positions):
                off = pl.multiple_of(plan.offset(half, position), 8)
                for at, (row, col) in enumerate(plan.pairs):
                    fmat[pl.ds(row * TILE + off, plan.rows), col * TILE : (col + 1) * TILE] = packed[half][
                        position, at * plan.rows : (at + 1) * plan.rows, :
                    ]
        for row, col in plan.pairs:
            if row != col:
                rs, cs = slice(row * TILE, (row + 1) * TILE), slice(col * TILE, (col + 1) * TILE)
                fmat[cs, rs] = fmat[rs, cs].T
        zmat[...] = jnp.dot(
            rsum_ref[...], fmat[...], precision=lax.Precision.HIGHEST, preferred_element_type=jnp.float32
        ) * (1.0 / total)

    shift = zmat[pl.ds(pair, 1), :]
    rsum = rsum_ref[pl.ds(pair, 1), :]
    grand = jnp.sum(shift * (0.5 * rsum - 1.0), axis=1, keepdims=True)
    key = k_ref[0]
    for part in range(length // TILE):
        rows = slice(part * TILE, (part + 1) * TILE)
        probs = probs_ref[0, rows, :].astype(jnp.float32)
        raised = probs * (fmat[rows, :] - shift)
        rowtotal = jnp.sum(raised, axis=1, keepdims=True)
        grand = grand + jnp.sum(rowtotal, axis=0, keepdims=True)
        dscores = (raised - probs * rowtotal).astype(jnp.bfloat16)
        dmat[rows, :] = dscores
        qgrad = jnp.dot(dscores, key, preferred_element_type=jnp.float32)
        qg_ref[0, rows, :] = (qgrad * (weight * scale)).astype(jnp.bfloat16)
    kgrad = lax.dot_general(
        dmat[...], q_ref[0], (((0,), (0,)), ((), ())), preferred_element_type=jnp.float32
    )
    kg_ref[0] = (kgrad * (weight * scale)).astype(jnp.bfloat16)
    wg_ref[pair // slot_count, pair % slot_count] = grand[0, 0]


def target_kernel(plan, mine_ref, other_ref, own_ref, send_ref):
    head = lax.axis_index("head")
    core, y_at, plane = head % 2, (head // 2) % 2, head // 4
    layer = lax.axis_index("layer")
    mine = mine_ref[...].astype(jnp.float32)
    other = other_ref[...].astype(jnp.float32)
    both = jnp.where(core == 0, jnp.concatenate([mine, other], 0), jnp.concatenate([other, mine], 0))
    blank = jnp.zeros_like(both)
    lanes = jnp.where(y_at == 0, jnp.concatenate([both, blank], 0), jnp.concatenate([blank, both], 0))
    for col in range(plan.blocks):
        flipped = lanes[:, col * TILE : (col + 1) * TILE].T
        gap = (col - plane + plan.blocks) % plan.blocks
        natural = (2 * gap < plan.blocks) | ((2 * gap == plan.blocks) & (plane < col))
        keep_natural = jnp.where(natural, 1.0, 0.0)
        keep_flipped = jnp.where(natural & (gap != 0), 0.0, 1.0)
        own = jnp.zeros((plan.rows, TILE), jnp.float32)
        send = jnp.zeros((plan.rows, TILE), jnp.float32)
        for unit in range(TILE // plan.rows):
            part = flipped[unit * plan.rows : (unit + 1) * plan.rows, :]
            own = jnp.where(unit == (2 * y_at + core) * plan.layers + layer, part, own)
            send = jnp.where(unit == (2 * (1 - y_at) + core) * plan.layers + layer, part, send)
        natural_part = jnp.zeros((plan.rows, TILE), jnp.float32)
        for unit in range(plan.layers):
            part = mine[unit * plan.rows : (unit + 1) * plan.rows, col * TILE : (col + 1) * TILE]
            natural_part = jnp.where(unit == layer, part, natural_part)
        own_ref[col * plan.rows : (col + 1) * plan.rows, :] = own * keep_flipped + natural_part * keep_natural
        send_ref[col * plan.rows : (col + 1) * plan.rows, :] = send * keep_flipped


def swap(value, axis, size, flip):
    return lax.ppermute(value, axis, [(i, i ^ flip) for i in range(size)])


def across(value, layers, heads, layer_flip, head_flip):
    if layer_flip == 0:
        return swap(value, "head", heads, head_flip)
    if head_flip == 0:
        return swap(value, "layer", layers, layer_flip)
    pairs = [
        (la * heads + he, (la ^ layer_flip) * heads + (he ^ head_flip)) for la in range(layers) for he in range(heads)
    ]
    return lax.ppermute(value, ("layer", "head"), pairs)


def exchange_fast(plan, packed, target):
    layers, heads, rows, blocks = plan.layers, plan.heads, plan.rows, plan.blocks
    other = swap(target, "head", heads, 1)
    share = jax.ShapeDtypeStruct((blocks * rows, TILE), jnp.float32)
    tsym, tsend = pl.pallas_call(
        functools.partial(target_kernel, plan), out_shape=(share, share), name="target_share"
    )(target, other)
    chip = packed[0] + swap(packed[1], "head", heads, 1)
    size = len(plan.pairs) * rows
    got = []
    for position in range(1, plan.positions):
        value = chip[position]
        if position == 1:
            value = jnp.concatenate([value, tsend], axis=0)
        got.append(across(value, layers, heads, position // 2, 2 * (position % 2)))
    tsym = tsym + got[0][size:]
    total = chip[0]
    for value in got:
        total = total + value[:size]
    planes = [tsym]
    flip = 1
    while flip < blocks:
        sent = jnp.concatenate([total] + planes, axis=0)
        came = swap(sent, "head", heads, 4 * flip)
        total = total + came[:size]
        step = blocks * rows
        planes = planes + [came[size + i * step : size + (i + 1) * step] for i in range(flip)]
        flip = 2 * flip
    plane = lax.axis_index("head") // 4

    def shared(row, col):
        value = planes[0]
        for flip in range(1, blocks):
            value = jnp.where((plane ^ flip) == row, planes[flip], value)
        return value[col * rows : (col + 1) * rows]

    tparts = []
    for row, col in plan.pairs:
        tparts.append(shared(row, col) if row == col else shared(row, col) + shared(col, row))
    error = 2.0 * jax.nn.sigmoid(total) - jnp.concatenate(tparts, axis=0)
    parts = [error]
    for position in range(1, plan.positions):
        parts.append(across(error, layers, heads, position // 2, 2 * (position % 2)))
    mine = jnp.stack(parts)
    return mine, swap(mine, "head", heads, 1)


def exchange_general(plan, packed, target):
    logit = lax.psum(packed[0][0], ("layer", "head"))
    whole = lax.all_gather(target, "head", axis=0, tiled=True)
    whole = (whole + whole.T).astype(jnp.float32)
    parts = [whole[r * TILE : (r + 1) * TILE, c * TILE : (c + 1) * TILE] for r, c in plan.pairs]
    return ((2.0 * jax.nn.sigmoid(logit) - jnp.concatenate(parts, axis=0))[None],)


def on_device(layers, heads_axis, queries, keys, head_weight, slot_head, target):
    layer_count, slot_count, length, size = queries.shape
    heads = head_weight.shape[1]
    count = layer_count * slot_count
    plan = Plan(layers, heads_axis, length)
    flat_q = queries.reshape(count, length, size)
    flat_k = keys.reshape(count, length, size)
    smem = pl.BlockSpec(memory_space=pltpu.SMEM)
    vectors = pl.BlockSpec((1, length, size), lambda i: (i, 0, 0))
    maps = pl.BlockSpec((1, length, length), lambda i: (i, 0, 0))
    packed_shape = (plan.positions, len(plan.pairs) * plan.rows, TILE)
    packed_spec = pl.BlockSpec(packed_shape, lambda i: (0, 0, 0))
    sums_shape = (pad8(count), length)
    sums_spec = pl.BlockSpec(sums_shape, lambda i: (0, 0))
    fwd = pl.pallas_call(
        functools.partial(forward_kernel, plan, slot_count, heads, count),
        grid=(count,),
        in_specs=[smem, smem, vectors, vectors],
        out_specs=[packed_spec] * plan.halves + [maps, sums_spec],
        out_shape=[jax.ShapeDtypeStruct(packed_shape, jnp.float32)] * plan.halves
        + [
            jax.ShapeDtypeStruct((count, length, length), jnp.bfloat16),
            jax.ShapeDtypeStruct(sums_shape, jnp.float32),
        ],
        scratch_shapes=[pltpu.VMEM((length, length), jnp.float32), pltpu.VMEM(sums_shape, jnp.float32)],
        compiler_params=pltpu.CompilerParams(vmem_limit_bytes=24 * 2**20),
        name="forward_maps",
    )(head_weight, slot_head, flat_q, flat_k)
    packed, probs, rsum = fwd[: plan.halves], fwd[plan.halves], fwd[plan.halves + 1]
    errors = (exchange_fast if plan.fast else exchange_general)(plan, packed, target)
    qgrad, kgrad, wgrad = pl.pallas_call(
        functools.partial(backward_kernel, plan, slot_count, heads, count),
        grid=(count,),
        in_specs=[smem, smem, vectors, vectors, maps, sums_spec] + [packed_spec] * plan.halves,
        out_specs=[vectors, vectors, smem],
        out_shape=[
            jax.ShapeDtypeStruct((count, length, size), jnp.bfloat16),
            jax.ShapeDtypeStruct((count, length, size), jnp.bfloat16),
            jax.ShapeDtypeStruct((layer_count, slot_count), jnp.float32),
        ],
        scratch_shapes=[
            pltpu.VMEM((length, length), jnp.float32),
            pltpu.VMEM(sums_shape, jnp.float32),
            pltpu.VMEM((length, length), jnp.bfloat16),
        ],
        compiler_params=pltpu.CompilerParams(vmem_limit_bytes=24 * 2**20),
        name="backward_maps",
    )(head_weight, slot_head, flat_q, flat_k, probs, rsum, *errors)
    return qgrad.reshape(queries.shape), kgrad.reshape(queries.shape), wgrad


def solution(mesh):
    return jax.shard_map(
        functools.partial(on_device, mesh.shape["layer"], mesh.shape["head"]),
        mesh=mesh,
        in_specs=(
            P("layer", "head", None, None),
            P("layer", "head", None, None),
            P("layer", None),
            P("head"),
            P("head", None),
        ),
        out_specs=(
            P("layer", "head", None, None),
            P("layer", "head", None, None),
            P("layer", "head"),
        ),
        check_vma=False,
    )
```

```python
import functools

import jax
import jax.numpy as jnp
from jax import lax
from jax.experimental import pallas as pl
from jax.experimental.pallas import tpu as pltpu
from jax.sharding import PartitionSpec as P

TILE = 128
FCHUNK = 128
BCHUNK = 128


def block_pairs(count):
    pairs = []
    for row in range(count):
        for col in range(count):
            gap = (col - row) % count
            if 2 * gap < count or (2 * gap == count and row < col):
                pairs.append((row, col))
    return pairs


def pad8(count):
    return -(-count // 8) * 8


def split3(value):
    first = value.astype(jnp.bfloat16).astype(jnp.float32)
    rest = value - first
    second = rest.astype(jnp.bfloat16).astype(jnp.float32)
    return first, second, rest - second


def pair_weight(hw_ref, head_ref, pair, slot_count, heads):
    layer, slot = pair // slot_count, pair % slot_count
    held = head_ref[slot]
    return jnp.where(held < heads, hw_ref[layer, jnp.minimum(held, heads - 1)], 0.0)


class Plan:
    def __init__(self, layers, heads, length):
        self.blocks = length // TILE
        self.pairs = block_pairs(self.blocks)
        self.layers, self.heads = layers, heads
        self.fast = (
            heads % 4 == 0
            and heads // 4 == self.blocks
            and self.blocks & (self.blocks - 1) == 0
            and layers & (layers - 1) == 0
            and (TILE // (4 * layers)) % 8 == 0
        )
        self.halves = 2 if self.fast else 1
        self.positions = 2 * layers if self.fast else 1
        self.rows = TILE // (self.halves * self.positions)
        self.size = len(self.pairs) * self.rows
        self.share = self.blocks * self.rows if self.fast else 0

    def start(self, position):
        return position * self.size + min(position, 2) * self.share

    def offset(self, half, position):
        if not self.fast:
            return 0
        head = lax.axis_index("head")
        core = (head % 2) ^ half
        y_at = ((head // 2) % 2) ^ (position % 2)
        layer = lax.axis_index("layer") ^ (position // 2)
        return ((2 * y_at + core) * self.layers + layer) * self.rows


def fetch(source, target, sem):
    copy = pltpu.make_async_copy(source, target, sem)
    copy.start()
    return copy


def forward_kernel(plan, dims, hw_hbm, head_hbm, t_hbm, q_hbm, k_hbm, *rest):
    layer_count, slot_count, heads = dims
    count = layer_count * slot_count
    outs, probs_hbm, rsum_ref = rest[: plan.halves], rest[plan.halves], rest[plan.halves + 1]
    hw_ref, head_ref, t_ref, q_ref, k_ref, p_ref, acc, scaled, flip, sems, qsem, ksem, psem = rest[plan.halves + 2 :]
    length = q_ref.shape[1]
    scale = q_ref.shape[2] ** (-0.5)
    total = 2.0 * length
    q_copies, k_copies, p_copies = [], [], []
    for pair in range(count):
        q_copies.append(fetch(q_hbm.at[pair], q_ref.at[pair], qsem.at[pair]))
        k_copies.append(fetch(k_hbm.at[pair], k_ref.at[pair], ksem.at[pair]))
        if pair == 0:
            head_copy = fetch(head_hbm, head_ref, sems.at[1])
            hw_copy = fetch(hw_hbm, hw_ref, sems.at[0])
            t_copy = fetch(t_hbm, t_ref, sems.at[2])
    scaled[...] = jnp.zeros_like(scaled)
    rsum_ref[...] = jnp.zeros_like(rsum_ref)
    head_copy.wait()
    hw_copy.wait()
    if plan.fast:
        target_share(plan, t_ref, t_copy, flip, outs)
    else:
        t_copy.wait()
    for pair in range(count):
        q_copies[pair].wait()
        k_copies[pair].wait()
        weight = pair_weight(hw_ref, head_ref, pair, slot_count, heads)
        colsum = jnp.zeros((8, length), jnp.float32)
        key = k_ref[pair]
        for part in range(length // FCHUNK):
            rows = slice(part * FCHUNK, (part + 1) * FCHUNK)
            scores = lax.dot_general(
                q_ref[pair, rows, :], key, (((1,), (1,)), ((), ())), preferred_element_type=jnp.float32
            )
            highest = jnp.max(scores, axis=1, keepdims=True)
            expo = jnp.exp((scores - highest) * scale)
            probs = expo * (1.0 / jnp.sum(expo, axis=1, keepdims=True))
            p_ref[pair, rows, :] = probs
            if pair == 0:
                acc[rows, :] = weight * probs
            else:
                acc[rows, :] += weight * probs
            colsum = colsum + jnp.sum(probs.reshape(FCHUNK // 8, 8, length), axis=0)
        p_copies.append(fetch(p_ref.at[pair], probs_hbm.at[pair], psem.at[pair]))
        rowsum = 1.0 + jnp.sum(colsum, axis=0, keepdims=True)
        rsum_ref[pair : pair + 1, :] = rowsum
        scaled[pair : pair + 1, :] = rowsum * (-weight / total)

    left = split3(scaled[...])
    right = split3(rsum_ref[...])
    order = ((0, 0), (0, 1), (1, 0), (1, 1), (0, 2), (2, 0))
    lefts = jnp.concatenate([left[a] for a, _ in order], axis=0).astype(jnp.bfloat16)
    rights = jnp.concatenate([right[b] for _, b in order], axis=0).astype(jnp.bfloat16)
    for row, col in plan.pairs:
        rs, cs = slice(row * TILE, (row + 1) * TILE), slice(col * TILE, (col + 1) * TILE)
        both = acc[rs, cs] + acc[cs, rs].T
        acc[rs, cs] = both + lax.dot_general(
            lefts[:, rs], rights[:, cs], (((0,), (0,)), ((), ())), preferred_element_type=jnp.float32
        )
    for half in range(plan.halves):
        for position in range(plan.positions):
            off = pl.multiple_of(plan.offset(half, position), 8)
            for at, (row, col) in enumerate(plan.pairs):
                start = plan.start(position) + at * plan.rows
                outs[half][start : start + plan.rows, :] = acc[
                    pl.ds(row * TILE + off, plan.rows), col * TILE : (col + 1) * TILE
                ]
    for copy in p_copies:
        copy.wait()


def target_share(plan, t_ref, t_copy, flip, outs):
    head = lax.axis_index("head")
    core, y_at, plane = head % 2, (head // 2) % 2, head // 4
    strip = TILE // 4
    flip[...] = jnp.zeros_like(flip)
    t_copy.wait()
    flip[pl.ds(pl.multiple_of(strip * (2 * y_at + core), 8), strip), :] = t_ref[...].astype(jnp.float32)
    natural = pl.multiple_of(plan.offset(0, 0), 8)
    for col in range(plan.blocks):
        gap = (col - plane + plan.blocks) % plan.blocks
        is_natural = (2 * gap < plan.blocks) | ((2 * gap == plan.blocks) & (plane < col))
        keep_natural = jnp.where(is_natural, 1.0, 0.0)
        keep_flipped = jnp.where(is_natural & (gap != 0), 0.0, 1.0)
        cols = slice(col * TILE, (col + 1) * TILE)
        straight = flip[pl.ds(natural, plan.rows), cols] * keep_natural
        turned = (flip[:, cols] * keep_flipped).T
        flip[:, cols] = turned
        for half in range(plan.halves):
            for position in range(2):
                off = pl.multiple_of(plan.offset(half, position), 8)
                start = plan.start(position) + len(plan.pairs) * plan.rows + col * plan.rows
                value = flip[pl.ds(off, plan.rows), cols]
                if half == 0 and position == 0:
                    value = value + straight
                outs[half][start : start + plan.rows, :] = value


def backward_kernel(plan, dims, hw_hbm, head_hbm, probs_hbm, q_ref, k_ref, rsum_ref, *rest):
    layer_count, slot_count, heads = dims
    count = layer_count * slot_count
    packed = rest[: plan.halves]
    qg_hbm, kg_hbm, wg_ref, hw_ref, head_ref, p_ref, fmat, dmat, qg_ref, kg_ref, sems, psem, qsem, ksem = rest[
        plan.halves :
    ]
    length = q_ref.shape[1]
    scale = q_ref.shape[2] ** (-0.5)
    total = 2.0 * length
    p_copies = []
    for pair in range(count):
        p_copies.append(fetch(probs_hbm.at[pair], p_ref.at[pair], psem.at[pair]))
        if pair == 0:
            head_copy = fetch(head_hbm, head_ref, sems.at[1])
            hw_copy = fetch(hw_hbm, hw_ref, sems.at[0])
    for half in range(plan.halves):
        for position in range(plan.positions):
            off = pl.multiple_of(plan.offset(half, position), 8)
            for at, (row, col) in enumerate(plan.pairs):
                fmat[pl.ds(row * TILE + off, plan.rows), col * TILE : (col + 1) * TILE] = packed[half][
                    position, at * plan.rows : (at + 1) * plan.rows, :
                ]
    for row, col in plan.pairs:
        if row != col:
            rs, cs = slice(row * TILE, (row + 1) * TILE), slice(col * TILE, (col + 1) * TILE)
            fmat[cs, rs] = fmat[rs, cs].T
    shifts = jnp.dot(
        rsum_ref[...], fmat[...], precision=lax.Precision.HIGHEST, preferred_element_type=jnp.float32
    ) * (1.0 / total)
    grands = jnp.sum(shifts * (0.5 * rsum_ref[...] - 1.0), axis=1, keepdims=True)
    head_copy.wait()
    hw_copy.wait()
    copies = []
    for pair in range(count):
        weight = pair_weight(hw_ref, head_ref, pair, slot_count, heads)
        shift = shifts[pair : pair + 1, :]
        key = k_ref[pair]
        p_copies[pair].wait()
        tops = jnp.zeros((8, 1), jnp.float32)
        for part in range(length // BCHUNK):
            rows = slice(part * BCHUNK, (part + 1) * BCHUNK)
            probs = p_ref[pair, rows, :]
            raised = probs * (fmat[rows, :] - shift)
            rowtotal = jnp.sum(raised, axis=1, keepdims=True)
            tops = tops + jnp.sum(rowtotal.reshape(BCHUNK // 8, 8, 1), axis=0)
            dscores = (weight * (raised - probs * rowtotal)).astype(jnp.bfloat16)
            dmat[rows, :] = dscores
            qgrad = jnp.dot(dscores, key, preferred_element_type=jnp.float32)
            qg_ref[pair, rows, :] = (qgrad * scale).astype(jnp.bfloat16)
        copies.append(fetch(qg_ref.at[pair], qg_hbm.at[pair], qsem.at[pair]))
        kgrad = lax.dot_general(
            dmat[...], q_ref[pair], (((0,), (0,)), ((), ())), preferred_element_type=jnp.float32
        )
        kg_ref[pair] = (kgrad * scale).astype(jnp.bfloat16)
        copies.append(fetch(kg_ref.at[pair], kg_hbm.at[pair], ksem.at[pair]))
        grand = grands[pair : pair + 1, :] + jnp.sum(tops, axis=0, keepdims=True)
        wg_ref[pair // slot_count, pair % slot_count] = grand[0, 0]
    for copy in copies:
        copy.wait()


def swap(value, axis, size, flip):
    return lax.ppermute(value, axis, [(i, i ^ flip) for i in range(size)])


def across(value, layers, heads, layer_flip, head_flip):
    if layer_flip == 0:
        return swap(value, "head", heads, head_flip)
    if head_flip == 0:
        return swap(value, "layer", layers, layer_flip)
    pairs = [
        (la * heads + he, (la ^ layer_flip) * heads + (he ^ head_flip)) for la in range(layers) for he in range(heads)
    ]
    return lax.ppermute(value, ("layer", "head"), pairs)


def exchange_fast(plan, packed):
    layers, heads, rows, blocks, size, share = plan.layers, plan.heads, plan.rows, plan.blocks, plan.size, plan.share
    chip = packed[0] + swap(packed[1], "head", heads, 1)
    got = []
    for position in range(1, plan.positions):
        value = chip[plan.start(position) : plan.start(position + 1)]
        got.append(across(value, layers, heads, position // 2, 2 * (position % 2)))
    tsym = chip[size : size + share] + got[0][size:]
    total = chip[:size]
    for value in got:
        total = total + value[:size]
    planes = {0: tsym}
    flip = blocks // 2
    while flip:
        order = sorted(planes)
        came = swap(jnp.concatenate([total] + [planes[i] for i in order], axis=0), "head", heads, 4 * flip)
        total = total + came[:size]
        for at, i in enumerate(order):
            planes[i ^ flip] = came[size + at * share : size + (at + 1) * share]
        flip = flip // 2
    plane = lax.axis_index("head") // 4

    def shared(row, col):
        value = planes[0]
        for flip in range(1, blocks):
            value = jnp.where((plane ^ flip) == row, planes[flip], value)
        return value[col * rows : (col + 1) * rows]

    tparts = []
    for row, col in plan.pairs:
        tparts.append(shared(row, col) if row == col else shared(row, col) + shared(col, row))
    error = 2.0 * jax.nn.sigmoid(total) - jnp.concatenate(tparts, axis=0)
    parts = [error]
    for position in range(1, plan.positions):
        parts.append(across(error, layers, heads, position // 2, 2 * (position % 2)))
    mine = jnp.stack(parts)
    return mine, swap(mine, "head", heads, 1)


def exchange_general(plan, packed, target):
    logit = lax.psum(packed[0], ("layer", "head"))
    whole = lax.all_gather(target, "head", axis=0, tiled=True)
    whole = (whole + whole.T).astype(jnp.float32)
    parts = [whole[r * TILE : (r + 1) * TILE, c * TILE : (c + 1) * TILE] for r, c in plan.pairs]
    return ((2.0 * jax.nn.sigmoid(logit) - jnp.concatenate(parts, axis=0))[None],)


def on_device(layers, heads_axis, queries, keys, head_weight, slot_head, target):
    layer_count, slot_count, length, size = queries.shape
    heads = head_weight.shape[1]
    count = layer_count * slot_count
    plan = Plan(layers, heads_axis, length)
    flat_q = queries.reshape(count, length, size)
    flat_k = keys.reshape(count, length, size)
    dims = (layer_count, slot_count, heads)
    hbm = pl.BlockSpec(memory_space=pltpu.HBM)
    vmem = pl.BlockSpec(memory_space=pltpu.VMEM)
    smem = pl.BlockSpec(memory_space=pltpu.SMEM)
    sums_shape = (pad8(count), length)
    params = pltpu.CompilerParams(vmem_limit_bytes=24 * 2**20)
    weights = [pltpu.SMEM(head_weight.shape, jnp.float32), pltpu.SMEM(slot_head.shape, jnp.int32)]
    pair_sems = pltpu.SemaphoreType.DMA((count,))
    fwd = pl.pallas_call(
        functools.partial(forward_kernel, plan, dims),
        in_specs=[hbm] * 5,
        out_specs=[vmem] * plan.halves + [hbm, vmem],
        out_shape=[jax.ShapeDtypeStruct((plan.start(plan.positions), TILE), jnp.float32)] * plan.halves
        + [
            jax.ShapeDtypeStruct((count, length, length), jnp.float32),
            jax.ShapeDtypeStruct(sums_shape, jnp.float32),
        ],
        scratch_shapes=weights
        + [
            pltpu.VMEM(target.shape, jnp.int32),
            pltpu.VMEM(flat_q.shape, jnp.bfloat16),
            pltpu.VMEM(flat_q.shape, jnp.bfloat16),
            pltpu.VMEM((count, length, length), jnp.float32),
            pltpu.VMEM((length, length), jnp.float32),
            pltpu.VMEM(sums_shape, jnp.float32),
            pltpu.VMEM((TILE, length), jnp.float32),
            pltpu.SemaphoreType.DMA((3,)),
            pair_sems,
            pair_sems,
            pair_sems,
        ],
        compiler_params=params,
        name="forward_maps",
    )(head_weight, slot_head, target, flat_q, flat_k)
    packed, probs, rsum = fwd[: plan.halves], fwd[plan.halves], fwd[plan.halves + 1]
    errors = exchange_fast(plan, packed) if plan.fast else exchange_general(plan, packed, target)
    qgrad, kgrad, wgrad = pl.pallas_call(
        functools.partial(backward_kernel, plan, dims),
        in_specs=[hbm, hbm, hbm] + [vmem] * (3 + plan.halves),
        out_specs=[hbm, hbm, smem],
        out_shape=[
            jax.ShapeDtypeStruct((count, length, size), jnp.bfloat16),
            jax.ShapeDtypeStruct((count, length, size), jnp.bfloat16),
            jax.ShapeDtypeStruct((layer_count, slot_count), jnp.float32),
        ],
        scratch_shapes=weights
        + [
            pltpu.VMEM((count, length, length), jnp.float32),
            pltpu.VMEM((length, length), jnp.float32),
            pltpu.VMEM((length, length), jnp.bfloat16),
            pltpu.VMEM(flat_q.shape, jnp.bfloat16),
            pltpu.VMEM(flat_q.shape, jnp.bfloat16),
            pltpu.SemaphoreType.DMA((2,)),
            pair_sems,
            pair_sems,
            pair_sems,
        ],
        compiler_params=params,
        name="backward_maps",
    )(head_weight, slot_head, probs, flat_q, flat_k, rsum, *errors)
    return qgrad.reshape(queries.shape), kgrad.reshape(queries.shape), wgrad


def solution(mesh):
    return jax.shard_map(
        functools.partial(on_device, mesh.shape["layer"], mesh.shape["head"]),
        mesh=mesh,
        in_specs=(
            P("layer", "head", None, None),
            P("layer", "head", None, None),
            P("layer", None),
            P("head"),
            P("head", None),
        ),
        out_specs=(
            P("layer", "head", None, None),
            P("layer", "head", None, None),
            P("layer", "head"),
        ),
        check_vma=False,
    )
```

```python
import functools

import jax
import jax.numpy as jnp
from jax import lax
from jax.experimental import pallas as pl
from jax.experimental.pallas import tpu as pltpu
from jax.sharding import PartitionSpec as P

TILE = 128
LOG2E = 1.4426950408889634
FCHUNK = 256
BCHUNK = 256


def block_pairs(count):
    pairs = []
    for row in range(count):
        for col in range(count):
            gap = (col - row) % count
            if 2 * gap < count or (2 * gap == count and row < col):
                pairs.append((row, col))
    return pairs


def group_of(count):
    return 3 if count % 3 == 0 else 2 if count % 2 == 0 else 1


def pad8(count):
    return -(-count // 8) * 8


def split3(value):
    first = value.astype(jnp.bfloat16).astype(jnp.float32)
    rest = value - first
    second = rest.astype(jnp.bfloat16).astype(jnp.float32)
    return first, second, rest - second


def pair_weight(hw_ref, head_ref, pair, slot_count, heads):
    layer, slot = pair // slot_count, pair % slot_count
    held = head_ref[slot]
    return jnp.where(held < heads, hw_ref[layer, jnp.minimum(held, heads - 1)], 0.0)


class Plan:
    def __init__(self, layers, heads, length):
        self.blocks = length // TILE
        self.pairs = block_pairs(self.blocks)
        self.layers, self.heads = layers, heads
        self.fast = (
            heads % 4 == 0
            and heads // 4 == self.blocks
            and self.blocks & (self.blocks - 1) == 0
            and layers & (layers - 1) == 0
            and (TILE // (4 * layers)) % 8 == 0
        )
        self.halves = 2 if self.fast else 1
        self.positions = 2 * layers if self.fast else 1
        self.rows = TILE // (self.halves * self.positions)
        self.size = len(self.pairs) * self.rows
        self.share = self.blocks * self.rows if self.fast else 0

    def start(self, position):
        return position * self.size + min(position, 2) * self.share

    def offset(self, half, position):
        if not self.fast:
            return 0
        head = lax.axis_index("head")
        core = (head % 2) ^ half
        y_at = ((head // 2) % 2) ^ (position % 2)
        layer = lax.axis_index("layer") ^ (position // 2)
        return ((2 * y_at + core) * self.layers + layer) * self.rows


def fetch(source, target, sem):
    copy = pltpu.make_async_copy(source, target, sem)
    copy.start()
    return copy


def softmax_rows(query, key):
    scores = lax.dot_general(query, key, (((1,), (1,)), ((), ())), preferred_element_type=jnp.float32)
    highest = jnp.max(scores, axis=1, keepdims=True)
    expo = jnp.exp2((scores - highest) * (LOG2E * query.shape[-1] ** (-0.5)))
    return expo * (1.0 / jnp.sum(expo, axis=1, keepdims=True))


def forward_kernel(plan, dims, hw_hbm, head_hbm, t_hbm, q_hbm, k_hbm, *rest):
    layer_count, slot_count, heads = dims
    count = layer_count * slot_count
    outs, rsum_ref = rest[: plan.halves], rest[plan.halves]
    hw_ref, head_ref, t_ref, q_ref, k_ref, acc, scaled, flip, sems, qsem, ksem = rest[plan.halves + 1 :]
    length = q_ref.shape[1]
    total = 2.0 * length
    q_copy = lambda pair: pltpu.make_async_copy(q_hbm.at[pair], q_ref.at[pair], qsem.at[pair])
    k_copy = lambda pair: pltpu.make_async_copy(k_hbm.at[pair], k_ref.at[pair], ksem.at[pair])
    for pair in range(count):
        q_copy(pair).start()
        k_copy(pair).start()
        if pair == 0:
            head_copy = fetch(head_hbm, head_ref, sems.at[1])
            hw_copy = fetch(hw_hbm, hw_ref, sems.at[0])
            t_copy = fetch(t_hbm, t_ref, sems.at[2])
    acc[...] = jnp.zeros_like(acc)
    scaled[...] = jnp.zeros_like(scaled)
    rsum_ref[...] = jnp.zeros_like(rsum_ref)
    head_copy.wait()
    hw_copy.wait()

    group = group_of(count)

    def several(step, carry):
        pairs = [step * group + i for i in range(group)]
        for pair in pairs:
            q_copy(pair).wait()
            k_copy(pair).wait()
        weights = [pair_weight(hw_ref, head_ref, pair, slot_count, heads) for pair in pairs]
        colsums = [jnp.zeros((8, length), jnp.float32) for _ in pairs]
        for part in range(length // FCHUNK):
            rows = slice(part * FCHUNK, (part + 1) * FCHUNK)
            added = acc[rows, :]
            for i, pair in enumerate(pairs):
                probs = softmax_rows(q_ref[pair, rows, :], k_ref[pair])
                added = added + weights[i] * probs
                colsums[i] = colsums[i] + jnp.sum(probs.reshape(FCHUNK // 8, 8, length), axis=0)
            acc[rows, :] = added
        for i, pair in enumerate(pairs):
            rowsum = 1.0 + jnp.sum(colsums[i], axis=0, keepdims=True)
            rsum_ref[pl.ds(pair, 1), :] = rowsum
            scaled[pl.ds(pair, 1), :] = rowsum * (-weights[i] / total)
        return carry

    lax.fori_loop(0, count // group, several, 0)
    if plan.fast:
        target_share(plan, t_ref, t_copy, flip, outs)
    else:
        t_copy.wait()
    left = split3(scaled[...])
    right = split3(rsum_ref[...])
    order = ((0, 0), (0, 1), (1, 0), (1, 1), (0, 2), (2, 0))
    lefts = jnp.concatenate([left[a] for a, _ in order], axis=0).astype(jnp.bfloat16)
    rights = jnp.concatenate([right[b] for _, b in order], axis=0).astype(jnp.bfloat16)
    for row, col in plan.pairs:
        rs, cs = slice(row * TILE, (row + 1) * TILE), slice(col * TILE, (col + 1) * TILE)
        both = acc[rs, cs] + acc[cs, rs].T
        acc[rs, cs] = both + lax.dot_general(
            lefts[:, rs], rights[:, cs], (((0,), (0,)), ((), ())), preferred_element_type=jnp.float32
        )
    for half in range(plan.halves):
        for position in range(plan.positions):
            off = pl.multiple_of(plan.offset(half, position), 8)
            for at, (row, col) in enumerate(plan.pairs):
                start = plan.start(position) + at * plan.rows
                outs[half][start : start + plan.rows, :] = acc[
                    pl.ds(row * TILE + off, plan.rows), col * TILE : (col + 1) * TILE
                ]


def target_share(plan, t_ref, t_copy, flip, outs):
    head = lax.axis_index("head")
    core, y_at, plane = head % 2, (head // 2) % 2, head // 4
    strip = TILE // 4
    flip[...] = jnp.zeros_like(flip)
    t_copy.wait()
    flip[pl.ds(pl.multiple_of(strip * (2 * y_at + core), 8), strip), :] = t_ref[...].astype(jnp.float32)
    natural = pl.multiple_of(plan.offset(0, 0), 8)
    for col in range(plan.blocks):
        gap = (col - plane + plan.blocks) % plan.blocks
        is_natural = (2 * gap < plan.blocks) | ((2 * gap == plan.blocks) & (plane < col))
        keep_natural = jnp.where(is_natural, 1.0, 0.0)
        keep_flipped = jnp.where(is_natural & (gap != 0), 0.0, 1.0)
        cols = slice(col * TILE, (col + 1) * TILE)
        straight = flip[pl.ds(natural, plan.rows), cols] * keep_natural
        turned = (flip[:, cols] * keep_flipped).T
        flip[:, cols] = turned
        for half in range(plan.halves):
            for position in range(2):
                off = pl.multiple_of(plan.offset(half, position), 8)
                start = plan.start(position) + len(plan.pairs) * plan.rows + col * plan.rows
                value = flip[pl.ds(off, plan.rows), cols]
                if half == 0 and position == 0:
                    value = value + straight
                outs[half][start : start + plan.rows, :] = value


def probs_kernel(q_ref, k_ref, error_ref, p_ref, own_ref):
    count, length = q_ref.shape[0], q_ref.shape[1]
    own_ref[...] = error_ref[...]

    group = group_of(count)

    def several(step, carry):
        for i in range(group):
            pair = step * group + i
            key = k_ref[pair]
            for part in range(length // FCHUNK):
                rows = slice(part * FCHUNK, (part + 1) * FCHUNK)
                p_ref[pair, rows, :] = softmax_rows(q_ref[pair, rows, :], key)
        return carry

    lax.fori_loop(0, count // group, several, 0)


def backward_kernel(plan, dims, hw_hbm, head_hbm, p_ref, q_ref, k_ref, rsum_ref, *rest):
    layer_count, slot_count, heads = dims
    count = layer_count * slot_count
    packed = rest[: plan.halves]
    qg_hbm, kg_hbm, wg_ref, hw_ref, head_ref, fmat, shift_ref, dmat, qg_ref, kg_ref, sems, qsem, ksem = rest[plan.halves :]
    length = q_ref.shape[1]
    scale = q_ref.shape[2] ** (-0.5)
    total = 2.0 * length
    q_copy = lambda pair: pltpu.make_async_copy(qg_ref.at[pair], qg_hbm.at[pair], qsem.at[pair])
    k_copy = lambda pair: pltpu.make_async_copy(kg_ref.at[pair], kg_hbm.at[pair], ksem.at[pair])
    head_copy = fetch(head_hbm, head_ref, sems.at[1])
    hw_copy = fetch(hw_hbm, hw_ref, sems.at[0])
    for half in range(plan.halves):
        for position in range(plan.positions):
            off = pl.multiple_of(plan.offset(half, position), 8)
            for at, (row, col) in enumerate(plan.pairs):
                fmat[pl.ds(row * TILE + off, plan.rows), col * TILE : (col + 1) * TILE] = packed[half][
                    position, at * plan.rows : (at + 1) * plan.rows, :
                ]
    for row, col in plan.pairs:
        if row != col:
            rs, cs = slice(row * TILE, (row + 1) * TILE), slice(col * TILE, (col + 1) * TILE)
            fmat[cs, rs] = fmat[rs, cs].T
    shifts = jnp.dot(
        rsum_ref[...], fmat[...], precision=lax.Precision.HIGHEST, preferred_element_type=jnp.float32
    ) * (1.0 / total)
    shift_ref[...] = shifts
    head_copy.wait()
    hw_copy.wait()

    group = group_of(count)

    def several(step, carry):
        pairs = [step * group + i for i in range(group)]
        for i, pair in enumerate(pairs):
            weight = pair_weight(hw_ref, head_ref, pair, slot_count, heads)
            shift = shift_ref[pl.ds(pair, 1), :]
            rowsum = rsum_ref[pl.ds(pair, 1), :]
            tops = jnp.zeros((8, 1), jnp.float32)
            for part in range(length // BCHUNK):
                rows = slice(part * BCHUNK, (part + 1) * BCHUNK)
                probs = p_ref[pair, rows, :]
                raised = probs * (fmat[rows, :] - shift)
                rowtotal = jnp.sum(raised, axis=1, keepdims=True)
                tops = tops + jnp.sum(rowtotal.reshape(BCHUNK // 8, 8, 1), axis=0)
                dmat[i, rows, :] = (weight * (raised - probs * rowtotal)).astype(jnp.bfloat16)
            qgrad = jnp.dot(dmat[i], k_ref[pair], preferred_element_type=jnp.float32)
            qg_ref[pair] = (qgrad * scale).astype(jnp.bfloat16)
            kgrad = lax.dot_general(
                dmat[i], q_ref[pair], (((0,), (0,)), ((), ())), preferred_element_type=jnp.float32
            )
            kg_ref[pair] = (kgrad * scale).astype(jnp.bfloat16)
            grand = jnp.sum(shift * (0.5 * rowsum - 1.0), axis=1, keepdims=True) + jnp.sum(
                tops, axis=0, keepdims=True
            )
            wg_ref[pair // slot_count, pair % slot_count] = grand[0, 0]
            q_copy(pair).start()
            k_copy(pair).start()
        return carry

    lax.fori_loop(0, count // group, several, 0)
    for pair in range(count):
        q_copy(pair).wait()
        k_copy(pair).wait()


def swap(value, axis, size, flip):
    return lax.ppermute(value, axis, [(i, i ^ flip) for i in range(size)])


def across(value, layers, heads, layer_flip, head_flip):
    if layer_flip == 0:
        return swap(value, "head", heads, head_flip)
    if head_flip == 0:
        return swap(value, "layer", layers, layer_flip)
    pairs = [
        (la * heads + he, (la ^ layer_flip) * heads + (he ^ head_flip)) for la in range(layers) for he in range(heads)
    ]
    return lax.ppermute(value, ("layer", "head"), pairs)


def exchange_fast(plan, packed, probs_of):
    layers, heads, rows, blocks, size, share = plan.layers, plan.heads, plan.rows, plan.blocks, plan.size, plan.share
    chip = packed[0] + swap(packed[1], "head", heads, 1)
    got = []
    for position in range(1, plan.positions):
        value = chip[plan.start(position) : plan.start(position + 1)]
        got.append(across(value, layers, heads, position // 2, 2 * (position % 2)))
    tsym = chip[size : size + share] + got[0][size:]
    total = chip[:size]
    for value in got:
        total = total + value[:size]
    planes = {0: tsym}
    flip = blocks // 2
    while flip:
        order = sorted(planes)
        came = swap(jnp.concatenate([total] + [planes[i] for i in order], axis=0), "head", heads, 4 * flip)
        total = total + came[:size]
        for at, i in enumerate(order):
            planes[i ^ flip] = came[size + at * share : size + (at + 1) * share]
        flip = flip // 2
    plane = lax.axis_index("head") // 4

    def shared(row, col):
        value = planes[0]
        for flip in range(1, blocks):
            value = jnp.where((plane ^ flip) == row, planes[flip], value)
        return value[col * rows : (col + 1) * rows]

    tparts = []
    for row, col in plan.pairs:
        tparts.append(shared(row, col) if row == col else shared(row, col) + shared(col, row))
    error = 2.0 * jax.nn.sigmoid(total) - jnp.concatenate(tparts, axis=0)
    parts = []
    for position in range(1, plan.positions):
        parts.append(across(error, layers, heads, position // 2, 2 * (position % 2)))
    probs, error = probs_of(error)
    mine = jnp.stack([error] + parts)
    return probs, (mine, swap(mine, "head", heads, 1))


def exchange_general(plan, packed, target, probs_of):
    logit = lax.psum(packed[0], ("layer", "head"))
    whole = lax.all_gather(target, "head", axis=0, tiled=True)
    whole = (whole + whole.T).astype(jnp.float32)
    parts = [whole[r * TILE : (r + 1) * TILE, c * TILE : (c + 1) * TILE] for r, c in plan.pairs]
    probs, error = probs_of(2.0 * jax.nn.sigmoid(logit) - jnp.concatenate(parts, axis=0))
    return probs, (error[None],)


def on_device(layers, heads_axis, queries, keys, head_weight, slot_head, target):
    layer_count, slot_count, length, size = queries.shape
    heads = head_weight.shape[1]
    count = layer_count * slot_count
    plan = Plan(layers, heads_axis, length)
    flat_q = queries.reshape(count, length, size)
    flat_k = keys.reshape(count, length, size)
    dims = (layer_count, slot_count, heads)
    hbm = pl.BlockSpec(memory_space=pltpu.HBM)
    vmem = pl.BlockSpec(memory_space=pltpu.VMEM)
    smem = pl.BlockSpec(memory_space=pltpu.SMEM)
    sums_shape = (pad8(count), length)
    params = pltpu.CompilerParams(vmem_limit_bytes=12 * 2**20)
    weights = [pltpu.SMEM(head_weight.shape, jnp.float32), pltpu.SMEM(slot_head.shape, jnp.int32)]
    pair_sems = pltpu.SemaphoreType.DMA((count,))
    head_weight, target_hbm, first_q, first_k = (
        pltpu.with_memory_space_constraint(value, pltpu.HBM) for value in (head_weight, target, flat_q, flat_k)
    )
    if slot_count > 1:
        slot_head = pltpu.with_memory_space_constraint(slot_head, pltpu.HBM)
    fwd = pl.pallas_call(
        functools.partial(forward_kernel, plan, dims),
        in_specs=[hbm] * 5,
        out_specs=[vmem] * (plan.halves + 1),
        out_shape=[pltpu.VMEM((plan.start(plan.positions), TILE), jnp.float32)] * plan.halves
        + [pltpu.VMEM(sums_shape, jnp.float32)],
        scratch_shapes=weights
        + [
            pltpu.VMEM(target.shape, jnp.int32),
            pltpu.VMEM(flat_q.shape, jnp.bfloat16),
            pltpu.VMEM(flat_q.shape, jnp.bfloat16),
            pltpu.VMEM((length, length), jnp.float32),
            pltpu.VMEM(sums_shape, jnp.float32),
            pltpu.VMEM((TILE, length), jnp.float32),
            pltpu.SemaphoreType.DMA((3,)),
            pair_sems,
            pair_sems,
        ],
        compiler_params=params,
        name="forward_maps",
    )(head_weight, slot_head, target_hbm, first_q, first_k)
    packed, rsum = fwd[: plan.halves], fwd[plan.halves]

    def probs_of(error):
        return pl.pallas_call(
            probs_kernel,
            in_specs=[vmem] * 3,
            out_specs=[vmem] * 2,
            out_shape=[pltpu.VMEM((count, length, length), jnp.float32), pltpu.VMEM(error.shape, jnp.float32)],
            compiler_params=params,
            cost_estimate=pl.CostEstimate(
                flops=2 * count * length * length * size,
                bytes_accessed=4 * count * length * length,
                transcendentals=count * length * length,
            ),
            name="probs_maps",
        )(flat_q, flat_k, error)

    if plan.fast:
        probs, errors = exchange_fast(plan, packed, probs_of)
    else:
        probs, errors = exchange_general(plan, packed, target, probs_of)
    qgrad, kgrad, wgrad = pl.pallas_call(
        functools.partial(backward_kernel, plan, dims),
        in_specs=[hbm] * 2 + [vmem] * (4 + plan.halves),
        out_specs=[hbm, hbm, smem],
        out_shape=[
            pltpu.HBM((count, length, size), jnp.bfloat16),
            pltpu.HBM((count, length, size), jnp.bfloat16),
            jax.ShapeDtypeStruct((layer_count, slot_count), jnp.float32),
        ],
        scratch_shapes=weights
        + [
            pltpu.VMEM((length, length), jnp.float32),
            pltpu.VMEM(sums_shape, jnp.float32),
            pltpu.VMEM((group_of(count), length, length), jnp.bfloat16),
            pltpu.VMEM(flat_q.shape, jnp.bfloat16),
            pltpu.VMEM(flat_q.shape, jnp.bfloat16),
            pltpu.SemaphoreType.DMA((2,)),
            pair_sems,
            pair_sems,
        ],
        compiler_params=params,
        name="backward_maps",
    )(head_weight, slot_head, probs, flat_q, flat_k, rsum, *errors)
    return qgrad.reshape(queries.shape), kgrad.reshape(queries.shape), wgrad


def solution(mesh):
    return jax.shard_map(
        functools.partial(on_device, mesh.shape["layer"], mesh.shape["head"]),
        mesh=mesh,
        in_specs=(
            P("layer", "head", None, None),
            P("layer", "head", None, None),
            P("layer", None),
            P("head"),
            P("head", None),
        ),
        out_specs=(
            P("layer", "head", None, None),
            P("layer", "head", None, None),
            P("layer", "head"),
        ),
        check_vma=False,
    )
```

```python
import functools

import jax
import jax.numpy as jnp
from jax import lax
from jax.experimental import pallas as pl
from jax.experimental.pallas import tpu as pltpu
from jax.sharding import PartitionSpec as P

TILE = 128
LOG2E = 1.4426950408889634
FCHUNK = 256
BCHUNK = 256


def block_pairs(count):
    pairs = []
    for row in range(count):
        for col in range(count):
            gap = (col - row) % count
            if 2 * gap < count or (2 * gap == count and row < col):
                pairs.append((row, col))
    return pairs


def group_of(count):
    return 3 if count % 3 == 0 else 2 if count % 2 == 0 else 1


def pad8(count):
    return -(-count // 8) * 8


def split3(value):
    first = value.astype(jnp.bfloat16).astype(jnp.float32)
    rest = value - first
    second = rest.astype(jnp.bfloat16).astype(jnp.float32)
    return first, second, rest - second


def pair_weight(hw_ref, head_ref, pair, slot_count, heads):
    layer, slot = pair // slot_count, pair % slot_count
    held = head_ref[slot]
    return jnp.where(held < heads, hw_ref[layer, jnp.minimum(held, heads - 1)], 0.0)


class Plan:
    def __init__(self, layers, heads, length):
        self.blocks = length // TILE
        self.pairs = block_pairs(self.blocks)
        self.layers, self.heads = layers, heads
        self.fast = (
            heads % 4 == 0
            and heads // 4 == self.blocks
            and self.blocks & (self.blocks - 1) == 0
            and layers & (layers - 1) == 0
            and (TILE // (4 * layers)) % 8 == 0
        )
        self.halves = 2 if self.fast else 1
        self.positions = 2 * layers if self.fast else 1
        self.rows = TILE // (self.halves * self.positions)
        self.folds = [(i, i + 1) for i in range(0, self.blocks, 2)] if self.fast and self.blocks % 2 == 0 else []
        lower = [low for _, low in self.folds]
        self.sent = [(row, col) for row, col in self.pairs if row != col or row not in lower]
        self.extra = pad8(len(self.folds))
        self.size = len(self.sent) * self.rows + self.extra
        self.share = self.blocks * self.rows if self.fast else 0

    def start(self, position):
        return position * self.size + min(position, 2) * self.share

    def offset(self, half, position):
        if not self.fast:
            return 0
        head = lax.axis_index("head")
        core = (head % 2) ^ half
        y_at = ((head // 2) % 2) ^ (position % 2)
        layer = lax.axis_index("layer") ^ (position // 2)
        return ((2 * y_at + core) * self.layers + layer) * self.rows


def triangle():
    rows = lax.broadcasted_iota(jnp.int32, (TILE, TILE), 0)
    cols = lax.broadcasted_iota(jnp.int32, (TILE, TILE), 1)
    return cols >= rows, cols == rows


def fetch(source, target, sem):
    copy = pltpu.make_async_copy(source, target, sem)
    copy.start()
    return copy


def softmax_rows(query, key):
    scores = lax.dot_general(query, key, (((1,), (1,)), ((), ())), preferred_element_type=jnp.float32)
    highest = jnp.max(scores, axis=1, keepdims=True)
    expo = jnp.exp2((scores - highest) * (LOG2E * query.shape[-1] ** (-0.5)))
    return expo * (1.0 / jnp.sum(expo, axis=1, keepdims=True))


def forward_kernel(plan, dims, hw_hbm, head_hbm, t_hbm, q_hbm, k_hbm, *rest):
    layer_count, slot_count, heads = dims
    count = layer_count * slot_count
    outs, rsum_ref = rest[: plan.halves], rest[plan.halves]
    hw_ref, head_ref, t_ref, q_ref, k_ref, acc, scaled, flip, sems, qsem, ksem = rest[plan.halves + 1 :]
    length = q_ref.shape[1]
    total = 2.0 * length
    q_copy = lambda pair: pltpu.make_async_copy(q_hbm.at[pair], q_ref.at[pair], qsem.at[pair])
    k_copy = lambda pair: pltpu.make_async_copy(k_hbm.at[pair], k_ref.at[pair], ksem.at[pair])
    group = group_of(count)
    t_copy = fetch(t_hbm, t_ref, sems.at[2])
    for pair in range(count):
        q_copy(pair).start()
        k_copy(pair).start()
        if pair == group - 1:
            head_copy = fetch(head_hbm, head_ref, sems.at[1])
            hw_copy = fetch(hw_hbm, hw_ref, sems.at[0])
    acc[...] = jnp.zeros_like(acc)
    scaled[...] = jnp.zeros_like(scaled)
    rsum_ref[...] = jnp.zeros_like(rsum_ref)
    if plan.fast:
        target_share(plan, t_ref, t_copy, flip, outs)
    else:
        t_copy.wait()
    head_copy.wait()
    hw_copy.wait()

    def several(step, carry):
        pairs = [step * group + i for i in range(group)]
        for pair in pairs:
            q_copy(pair).wait()
            k_copy(pair).wait()
        weights = [pair_weight(hw_ref, head_ref, pair, slot_count, heads) for pair in pairs]
        colsums = [jnp.zeros((8, length), jnp.float32) for _ in pairs]
        for part in range(length // FCHUNK):
            rows = slice(part * FCHUNK, (part + 1) * FCHUNK)
            added = acc[rows, :]
            for i, pair in enumerate(pairs):
                probs = softmax_rows(q_ref[pair, rows, :], k_ref[pair])
                added = added + weights[i] * probs
                colsums[i] = colsums[i] + jnp.sum(probs.reshape(FCHUNK // 8, 8, length), axis=0)
            acc[rows, :] = added
        for i, pair in enumerate(pairs):
            rowsum = 1.0 + jnp.sum(colsums[i], axis=0, keepdims=True)
            rsum_ref[pl.ds(pair, 1), :] = rowsum
            scaled[pl.ds(pair, 1), :] = rowsum * (-weights[i] / total)
        return carry

    lax.fori_loop(0, count // group, several, 0)
    left = split3(scaled[...])
    right = split3(rsum_ref[...])
    order = ((0, 0), (0, 1), (1, 0), (1, 1), (0, 2), (2, 0))
    lefts = jnp.concatenate([left[a] for a, _ in order], axis=0).astype(jnp.bfloat16)
    rights = jnp.concatenate([right[b] for _, b in order], axis=0).astype(jnp.bfloat16)
    for row, col in plan.pairs:
        rs, cs = slice(row * TILE, (row + 1) * TILE), slice(col * TILE, (col + 1) * TILE)
        both = acc[rs, cs] + acc[cs, rs].T
        acc[rs, cs] = both + lax.dot_general(
            lefts[:, rs], rights[:, cs], (((0,), (0,)), ((), ())), preferred_element_type=jnp.float32
        )
    diagonals = []
    if plan.folds:
        upper, middle = triangle()
        for high, low in plan.folds:
            hs, ls = slice(high * TILE, (high + 1) * TILE), slice(low * TILE, (low + 1) * TILE)
            below = acc[ls, ls]
            acc[hs, hs] = jnp.where(upper, acc[hs, hs], below)
            diagonals.append(jnp.sum(jnp.where(middle, below, 0.0), axis=0, keepdims=True))
        diagonals.append(jnp.zeros((plan.extra - len(plan.folds), TILE), jnp.float32))
        diagonals = jnp.concatenate(diagonals, axis=0)
    for half in range(plan.halves):
        for position in range(plan.positions):
            off = pl.multiple_of(plan.offset(half, position), 8)
            for at, (row, col) in enumerate(plan.sent):
                start = plan.start(position) + at * plan.rows
                outs[half][start : start + plan.rows, :] = acc[
                    pl.ds(row * TILE + off, plan.rows), col * TILE : (col + 1) * TILE
                ]
            if plan.folds:
                start = plan.start(position) + len(plan.sent) * plan.rows
                outs[half][start : start + plan.extra, :] = diagonals


def target_share(plan, t_ref, t_copy, flip, outs):
    head = lax.axis_index("head")
    core, y_at, plane = head % 2, (head // 2) % 2, head // 4
    strip = TILE // 4
    flip[...] = jnp.zeros_like(flip)
    t_copy.wait()
    flip[pl.ds(pl.multiple_of(strip * (2 * y_at + core), 8), strip), :] = t_ref[...].astype(jnp.float32)
    natural = pl.multiple_of(plan.offset(0, 0), 8)
    for col in range(plan.blocks):
        gap = (col - plane + plan.blocks) % plan.blocks
        is_natural = (2 * gap < plan.blocks) | ((2 * gap == plan.blocks) & (plane < col))
        keep_natural = jnp.where(is_natural, 1.0, 0.0)
        keep_flipped = jnp.where(is_natural & (gap != 0), 0.0, 1.0)
        cols = slice(col * TILE, (col + 1) * TILE)
        straight = flip[pl.ds(natural, plan.rows), cols] * keep_natural
        turned = (flip[:, cols] * keep_flipped).T
        flip[:, cols] = turned
        for half in range(plan.halves):
            for position in range(2):
                off = pl.multiple_of(plan.offset(half, position), 8)
                start = plan.start(position) + plan.size + col * plan.rows
                value = flip[pl.ds(off, plan.rows), cols]
                if half == 0 and position == 0:
                    value = value + straight
                outs[half][start : start + plan.rows, :] = value


def probs_kernel(q_ref, k_ref, error_ref, p_ref, own_ref):
    count, length = q_ref.shape[0], q_ref.shape[1]
    own_ref[...] = error_ref[...]

    group = group_of(count)

    def several(step, carry):
        for i in range(group):
            pair = step * group + i
            key = k_ref[pair]
            for part in range(length // FCHUNK):
                rows = slice(part * FCHUNK, (part + 1) * FCHUNK)
                p_ref[pair, rows, :] = softmax_rows(q_ref[pair, rows, :], key)
        return carry

    lax.fori_loop(0, count // group, several, 0)


def backward_kernel(plan, dims, hw_hbm, head_hbm, p_ref, q_ref, k_ref, rsum_ref, *rest):
    layer_count, slot_count, heads = dims
    count = layer_count * slot_count
    packed = rest[: plan.halves]
    qg_hbm, kg_hbm, wg_ref, hw_ref, head_ref, fmat, shift_ref, dmat, qg_ref, kg_ref, sems, qsem, ksem = rest[plan.halves :]
    length = q_ref.shape[1]
    scale = q_ref.shape[2] ** (-0.5)
    total = 2.0 * length
    q_copy = lambda pair: pltpu.make_async_copy(qg_ref.at[pair], qg_hbm.at[pair], qsem.at[pair])
    k_copy = lambda pair: pltpu.make_async_copy(kg_ref.at[pair], kg_hbm.at[pair], ksem.at[pair])
    head_copy = fetch(head_hbm, head_ref, sems.at[1])
    hw_copy = fetch(hw_hbm, hw_ref, sems.at[0])
    lanes = lax.broadcasted_iota(jnp.int32, (plan.extra, TILE), 1) if plan.folds else None
    diagonals = 0.0
    for half in range(plan.halves):
        for position in range(plan.positions):
            off = pl.multiple_of(plan.offset(half, position), 8)
            if plan.folds:
                ends = packed[half][position, len(plan.sent) * plan.rows : plan.size, :]
                diagonals = diagonals + jnp.where((lanes >= off) & (lanes < off + plan.rows), ends, 0.0)
            for at, (row, col) in enumerate(plan.sent):
                fmat[pl.ds(row * TILE + off, plan.rows), col * TILE : (col + 1) * TILE] = packed[half][
                    position, at * plan.rows : (at + 1) * plan.rows, :
                ]
    if plan.folds:
        upper, middle = triangle()
        for at, (high, low) in enumerate(plan.folds):
            hs, ls = slice(high * TILE, (high + 1) * TILE), slice(low * TILE, (low + 1) * TILE)
            both = fmat[hs, hs]
            turned = both.T
            fmat[hs, hs] = jnp.where(upper, both, turned)
            fmat[ls, ls] = jnp.where(middle, diagonals[at : at + 1, :], jnp.where(upper, turned, both))
    for row, col in plan.pairs:
        if row != col:
            rs, cs = slice(row * TILE, (row + 1) * TILE), slice(col * TILE, (col + 1) * TILE)
            fmat[cs, rs] = fmat[rs, cs].T
    shifts = jnp.dot(
        rsum_ref[...], fmat[...], precision=lax.Precision.HIGHEST, preferred_element_type=jnp.float32
    ) * (1.0 / total)
    shift_ref[...] = shifts
    head_copy.wait()
    hw_copy.wait()

    group = group_of(count)

    def several(step, carry):
        pairs = [step * group + i for i in range(group)]
        for i, pair in enumerate(pairs):
            weight = pair_weight(hw_ref, head_ref, pair, slot_count, heads)
            shift = shift_ref[pl.ds(pair, 1), :]
            rowsum = rsum_ref[pl.ds(pair, 1), :]
            tops = jnp.zeros((8, 1), jnp.float32)
            for part in range(length // BCHUNK):
                rows = slice(part * BCHUNK, (part + 1) * BCHUNK)
                probs = p_ref[pair, rows, :]
                raised = probs * (fmat[rows, :] - shift)
                rowtotal = jnp.sum(raised, axis=1, keepdims=True)
                tops = tops + jnp.sum(rowtotal.reshape(BCHUNK // 8, 8, 1), axis=0)
                dmat[i, rows, :] = (weight * (raised - probs * rowtotal)).astype(jnp.bfloat16)
            qgrad = jnp.dot(dmat[i], k_ref[pair], preferred_element_type=jnp.float32)
            qg_ref[pair] = (qgrad * scale).astype(jnp.bfloat16)
            kgrad = lax.dot_general(
                q_ref[pair], dmat[i], (((0,), (0,)), ((), ())), preferred_element_type=jnp.float32
            )
            kg_ref[pair] = (kgrad.T * scale).astype(jnp.bfloat16)
            grand = jnp.sum(shift * (0.5 * rowsum - 1.0), axis=1, keepdims=True) + jnp.sum(
                tops, axis=0, keepdims=True
            )
            wg_ref[pair // slot_count, pair % slot_count] = grand[0, 0]
            q_copy(pair).start()
            k_copy(pair).start()
        return carry

    lax.fori_loop(0, count // group, several, 0)
    for pair in range(count):
        q_copy(pair).wait()
        k_copy(pair).wait()


def swap(value, axis, size, flip):
    return lax.ppermute(value, axis, [(i, i ^ flip) for i in range(size)])


def across(value, layers, heads, layer_flip, head_flip):
    if layer_flip == 0:
        return swap(value, "head", heads, head_flip)
    if head_flip == 0:
        return swap(value, "layer", layers, layer_flip)
    pairs = [
        (la * heads + he, (la ^ layer_flip) * heads + (he ^ head_flip)) for la in range(layers) for he in range(heads)
    ]
    return lax.ppermute(value, ("layer", "head"), pairs)


def exchange_fast(plan, packed, probs_of):
    layers, heads, rows, blocks, size, share = plan.layers, plan.heads, plan.rows, plan.blocks, plan.size, plan.share
    chip = packed[0] + swap(packed[1], "head", heads, 1)
    got = []
    for position in range(1, plan.positions):
        value = chip[plan.start(position) : plan.start(position + 1)]
        got.append(across(value, layers, heads, position // 2, 2 * (position % 2)))
    tsym = chip[size : size + share] + got[0][size:]
    total = chip[:size]
    for value in got:
        total = total + value[:size]
    planes = {0: tsym}
    flip = blocks // 2
    while flip:
        order = sorted(planes)
        came = swap(jnp.concatenate([total] + [planes[i] for i in order], axis=0), "head", heads, 4 * flip)
        total = total + came[:size]
        for at, i in enumerate(order):
            planes[i ^ flip] = came[size + at * share : size + (at + 1) * share]
        flip = flip // 2
    plane = lax.axis_index("head") // 4

    def shared(row, col):
        value = planes[0]
        for flip in range(1, blocks):
            value = jnp.where((plane ^ flip) == row, planes[flip], value)
        return value[col * rows : (col + 1) * rows]

    off = plan.offset(0, 0)
    lows = dict(plan.folds)
    at_row = lax.broadcasted_iota(jnp.int32, (rows, TILE), 0) + off
    at_col = lax.broadcasted_iota(jnp.int32, (rows, TILE), 1)
    tparts = []
    for row, col in plan.sent:
        if row != col:
            tparts.append(shared(row, col) + shared(col, row))
        elif row in lows:
            tparts.append(jnp.where(at_col >= at_row, shared(row, row), shared(lows[row], lows[row])))
        else:
            tparts.append(shared(row, row))
    if plan.folds:
        ends = [jnp.sum(jnp.where(at_col == at_row, shared(low, low), 0.0), axis=0, keepdims=True) for _, low in plan.folds]
        tparts.append(jnp.pad(jnp.concatenate(ends, axis=0), ((0, plan.extra - len(ends)), (0, 0))))
    error = 2.0 * jax.nn.sigmoid(total) - jnp.concatenate(tparts, axis=0)
    parts = []
    for position in range(1, plan.positions):
        parts.append(across(error, layers, heads, position // 2, 2 * (position % 2)))
    probs, error = probs_of(error)
    mine = jnp.stack([error] + parts)
    return probs, (mine, swap(mine, "head", heads, 1))


def exchange_general(plan, packed, target, probs_of):
    logit = lax.psum(packed[0], ("layer", "head"))
    whole = lax.all_gather(target, "head", axis=0, tiled=True)
    whole = (whole + whole.T).astype(jnp.float32)
    parts = [whole[r * TILE : (r + 1) * TILE, c * TILE : (c + 1) * TILE] for r, c in plan.pairs]
    probs, error = probs_of(2.0 * jax.nn.sigmoid(logit) - jnp.concatenate(parts, axis=0))
    return probs, (error[None],)


def on_device(layers, heads_axis, queries, keys, head_weight, slot_head, target):
    layer_count, slot_count, length, size = queries.shape
    heads = head_weight.shape[1]
    count = layer_count * slot_count
    plan = Plan(layers, heads_axis, length)
    flat_q = queries.reshape(count, length, size)
    flat_k = keys.reshape(count, length, size)
    dims = (layer_count, slot_count, heads)
    hbm = pl.BlockSpec(memory_space=pltpu.HBM)
    vmem = pl.BlockSpec(memory_space=pltpu.VMEM)
    smem = pl.BlockSpec(memory_space=pltpu.SMEM)
    sums_shape = (pad8(count), length)
    params = pltpu.CompilerParams(vmem_limit_bytes=12 * 2**20)
    weights = [pltpu.SMEM(head_weight.shape, jnp.float32), pltpu.SMEM(slot_head.shape, jnp.int32)]
    pair_sems = pltpu.SemaphoreType.DMA((count,))
    head_weight, target_hbm, first_q, first_k = (
        pltpu.with_memory_space_constraint(value, pltpu.HBM) for value in (head_weight, target, flat_q, flat_k)
    )
    if slot_count > 1:
        slot_head = pltpu.with_memory_space_constraint(slot_head, pltpu.HBM)
    fwd = pl.pallas_call(
        functools.partial(forward_kernel, plan, dims),
        in_specs=[hbm] * 5,
        out_specs=[vmem] * (plan.halves + 1),
        out_shape=[pltpu.VMEM((plan.start(plan.positions), TILE), jnp.float32)] * plan.halves
        + [pltpu.VMEM(sums_shape, jnp.float32)],
        scratch_shapes=weights
        + [
            pltpu.VMEM(target.shape, jnp.int32),
            pltpu.VMEM(flat_q.shape, jnp.bfloat16),
            pltpu.VMEM(flat_q.shape, jnp.bfloat16),
            pltpu.VMEM((length, length), jnp.float32),
            pltpu.VMEM(sums_shape, jnp.float32),
            pltpu.VMEM((TILE, length), jnp.float32),
            pltpu.SemaphoreType.DMA((3,)),
            pair_sems,
            pair_sems,
        ],
        compiler_params=params,
        name="forward_maps",
    )(head_weight, slot_head, target_hbm, first_q, first_k)
    packed, rsum = fwd[: plan.halves], fwd[plan.halves]

    def probs_of(error):
        return pl.pallas_call(
            probs_kernel,
            in_specs=[vmem] * 3,
            out_specs=[vmem] * 2,
            out_shape=[pltpu.VMEM((count, length, length), jnp.float32), pltpu.VMEM(error.shape, jnp.float32)],
            compiler_params=params,
            cost_estimate=pl.CostEstimate(
                flops=2 * count * length * length * size,
                bytes_accessed=4 * count * length * length,
                transcendentals=count * length * length,
            ),
            name="probs_maps",
        )(flat_q, flat_k, error)

    if plan.fast:
        probs, errors = exchange_fast(plan, packed, probs_of)
    else:
        probs, errors = exchange_general(plan, packed, target, probs_of)
    qgrad, kgrad, wgrad = pl.pallas_call(
        functools.partial(backward_kernel, plan, dims),
        in_specs=[hbm] * 2 + [vmem] * (4 + plan.halves),
        out_specs=[hbm, hbm, smem],
        out_shape=[
            pltpu.HBM((count, length, size), jnp.bfloat16),
            pltpu.HBM((count, length, size), jnp.bfloat16),
            jax.ShapeDtypeStruct((layer_count, slot_count), jnp.float32),
        ],
        scratch_shapes=weights
        + [
            pltpu.VMEM((length, length), jnp.float32),
            pltpu.VMEM(sums_shape, jnp.float32),
            pltpu.VMEM((group_of(count), length, length), jnp.bfloat16),
            pltpu.VMEM(flat_q.shape, jnp.bfloat16),
            pltpu.VMEM(flat_q.shape, jnp.bfloat16),
            pltpu.SemaphoreType.DMA((2,)),
            pair_sems,
            pair_sems,
        ],
        compiler_params=params,
        name="backward_maps",
    )(head_weight, slot_head, probs, flat_q, flat_k, rsum, *errors)
    return qgrad.reshape(queries.shape), kgrad.reshape(queries.shape), wgrad


def solution(mesh):
    return jax.shard_map(
        functools.partial(on_device, mesh.shape["layer"], mesh.shape["head"]),
        mesh=mesh,
        in_specs=(
            P("layer", "head", None, None),
            P("layer", "head", None, None),
            P("layer", None),
            P("head"),
            P("head", None),
        ),
        out_specs=(
            P("layer", "head", None, None),
            P("layer", "head", None, None),
            P("layer", "head"),
        ),
        check_vma=False,
    )
```

```python
import functools

import jax
import jax.numpy as jnp
from jax import lax
from jax.experimental import pallas as pl
from jax.experimental.pallas import tpu as pltpu
from jax.sharding import PartitionSpec as P

TILE = 128
LOG2E = 1.4426950408889634
FCHUNK = 256
BCHUNK = 256


def block_pairs(count):
    pairs = []
    for row in range(count):
        for col in range(count):
            gap = (col - row) % count
            if 2 * gap < count or (2 * gap == count and row < col):
                pairs.append((row, col))
    return pairs


def group_of(count):
    return 3 if count % 3 == 0 else 2 if count % 2 == 0 else 1


def pad8(count):
    return -(-count // 8) * 8


def split3(value):
    first = value.astype(jnp.bfloat16).astype(jnp.float32)
    rest = value - first
    second = rest.astype(jnp.bfloat16).astype(jnp.float32)
    return first, second, rest - second


def pair_weight(hw_ref, head_ref, pair, slot_count, heads):
    layer, slot = pair // slot_count, pair % slot_count
    held = head_ref[slot]
    return jnp.where(held < heads, hw_ref[layer, jnp.minimum(held, heads - 1)], 0.0)


class Plan:
    def __init__(self, layers, heads, length):
        self.blocks = length // TILE
        self.pairs = block_pairs(self.blocks)
        self.layers, self.heads = layers, heads
        self.fast = (
            heads % 4 == 0
            and heads // 4 == self.blocks
            and self.blocks & (self.blocks - 1) == 0
            and layers & (layers - 1) == 0
            and (TILE // (4 * layers)) % 8 == 0
        )
        self.halves = 2 if self.fast else 1
        self.positions = 2 * layers if self.fast else 1
        self.rows = TILE // (self.halves * self.positions)
        self.folds = [(i, i + 1) for i in range(0, self.blocks, 2)] if self.fast and self.blocks % 2 == 0 else []
        lower = [low for _, low in self.folds]
        self.sent = [(row, col) for row, col in self.pairs if row != col or row not in lower]
        self.extra = pad8(len(self.folds))
        self.size = len(self.sent) * self.rows + self.extra
        self.share = self.blocks * self.rows if self.fast else 0

    def start(self, position):
        return position * self.size + min(position, 2) * self.share

    def offset(self, half, position):
        if not self.fast:
            return 0
        head = lax.axis_index("head")
        core = (head % 2) ^ half
        y_at = ((head // 2) % 2) ^ (position % 2)
        layer = lax.axis_index("layer") ^ (position // 2)
        return ((2 * y_at + core) * self.layers + layer) * self.rows


def triangle():
    rows = lax.broadcasted_iota(jnp.int32, (TILE, TILE), 0)
    cols = lax.broadcasted_iota(jnp.int32, (TILE, TILE), 1)
    return cols >= rows, cols == rows


def fetch(source, target, sem):
    copy = pltpu.make_async_copy(source, target, sem)
    copy.start()
    return copy


def softmax_rows(query, key):
    scores = lax.dot_general(query, key, (((1,), (1,)), ((), ())), preferred_element_type=jnp.float32)
    highest = jnp.max(scores, axis=1, keepdims=True)
    expo = jnp.exp2((scores - highest) * (LOG2E * query.shape[-1] ** (-0.5)))
    return expo * (1.0 / jnp.sum(expo, axis=1, keepdims=True))


def forward_kernel(plan, dims, hw_hbm, head_hbm, t_hbm, q_hbm, k_hbm, *rest):
    layer_count, slot_count, heads = dims
    count = layer_count * slot_count
    outs, rsum_ref = rest[: plan.halves], rest[plan.halves]
    hw_ref, head_ref, t_ref, q_ref, k_ref, acc, scaled, flip, sems, qsem, ksem = rest[plan.halves + 1 :]
    length = q_ref.shape[1]
    total = 2.0 * length
    q_copy = lambda pair: pltpu.make_async_copy(q_hbm.at[pair], q_ref.at[pair], qsem.at[pair])
    k_copy = lambda pair: pltpu.make_async_copy(k_hbm.at[pair], k_ref.at[pair], ksem.at[pair])
    group = group_of(count)
    t_copy = fetch(t_hbm, t_ref, sems.at[2])
    for pair in range(count):
        q_copy(pair).start()
        k_copy(pair).start()
        if pair == group - 1:
            head_copy = fetch(head_hbm, head_ref, sems.at[1])
            hw_copy = fetch(hw_hbm, hw_ref, sems.at[0])
    acc[...] = jnp.zeros_like(acc)
    scaled[...] = jnp.zeros_like(scaled)
    rsum_ref[...] = jnp.zeros_like(rsum_ref)
    if plan.fast:
        target_share(plan, t_ref, t_copy, flip, outs)
    else:
        t_copy.wait()
    head_copy.wait()
    hw_copy.wait()

    def several(step, carry):
        pairs = [step * group + i for i in range(group)]
        for pair in pairs:
            q_copy(pair).wait()
            k_copy(pair).wait()
        weights = [pair_weight(hw_ref, head_ref, pair, slot_count, heads) for pair in pairs]
        colsums = [jnp.zeros((8, length), jnp.float32) for _ in pairs]
        for part in range(length // FCHUNK):
            rows = slice(part * FCHUNK, (part + 1) * FCHUNK)
            added = acc[rows, :]
            for i, pair in enumerate(pairs):
                probs = softmax_rows(q_ref[pair, rows, :], k_ref[pair])
                added = added + weights[i] * probs
                colsums[i] = colsums[i] + jnp.sum(probs.reshape(FCHUNK // 8, 8, length), axis=0)
            acc[rows, :] = added
        for i, pair in enumerate(pairs):
            rowsum = 1.0 + jnp.sum(colsums[i], axis=0, keepdims=True)
            rsum_ref[pl.ds(pair, 1), :] = rowsum
            scaled[pl.ds(pair, 1), :] = rowsum * (-weights[i] / total)
        return carry

    lax.fori_loop(0, count // group, several, 0)
    left = split3(scaled[...])
    right = split3(rsum_ref[...])
    order = ((0, 0), (0, 1), (1, 0), (1, 1), (0, 2), (2, 0))
    lefts = jnp.concatenate([left[a] for a, _ in order], axis=0).astype(jnp.bfloat16)
    rights = jnp.concatenate([right[b] for _, b in order], axis=0).astype(jnp.bfloat16)
    for row, col in plan.pairs:
        rs, cs = slice(row * TILE, (row + 1) * TILE), slice(col * TILE, (col + 1) * TILE)
        both = acc[rs, cs] + acc[cs, rs].T
        acc[rs, cs] = both + lax.dot_general(
            lefts[:, rs], rights[:, cs], (((0,), (0,)), ((), ())), preferred_element_type=jnp.float32
        )
    diagonals = []
    if plan.folds:
        upper, middle = triangle()
        for high, low in plan.folds:
            hs, ls = slice(high * TILE, (high + 1) * TILE), slice(low * TILE, (low + 1) * TILE)
            below = acc[ls, ls]
            acc[hs, hs] = jnp.where(upper, acc[hs, hs], below)
            diagonals.append(jnp.sum(jnp.where(middle, below, 0.0), axis=0, keepdims=True))
        diagonals.append(jnp.zeros((plan.extra - len(plan.folds), TILE), jnp.float32))
        diagonals = jnp.concatenate(diagonals, axis=0)
    for half in range(plan.halves):
        for position in range(plan.positions):
            off = pl.multiple_of(plan.offset(half, position), 8)
            for at, (row, col) in enumerate(plan.sent):
                start = plan.start(position) + at * plan.rows
                outs[half][start : start + plan.rows, :] = acc[
                    pl.ds(row * TILE + off, plan.rows), col * TILE : (col + 1) * TILE
                ]
            if plan.folds:
                start = plan.start(position) + len(plan.sent) * plan.rows
                outs[half][start : start + plan.extra, :] = diagonals


def target_share(plan, t_ref, t_copy, flip, outs):
    head = lax.axis_index("head")
    core, y_at, plane = head % 2, (head // 2) % 2, head // 4
    strip = TILE // 4
    flip[...] = jnp.zeros_like(flip)
    t_copy.wait()
    flip[pl.ds(pl.multiple_of(strip * (2 * y_at + core), 8), strip), :] = t_ref[...].astype(jnp.float32)
    natural = pl.multiple_of(plan.offset(0, 0), 8)
    for col in range(plan.blocks):
        gap = (col - plane + plan.blocks) % plan.blocks
        is_natural = (2 * gap < plan.blocks) | ((2 * gap == plan.blocks) & (plane < col))
        keep_natural = jnp.where(is_natural, 1.0, 0.0)
        keep_flipped = jnp.where(is_natural & (gap != 0), 0.0, 1.0)
        cols = slice(col * TILE, (col + 1) * TILE)
        straight = flip[pl.ds(natural, plan.rows), cols] * keep_natural
        turned = (flip[:, cols] * keep_flipped).T
        flip[:, cols] = turned
        for half in range(plan.halves):
            for position in range(2):
                off = pl.multiple_of(plan.offset(half, position), 8)
                start = plan.start(position) + plan.size + col * plan.rows
                value = flip[pl.ds(off, plan.rows), cols]
                if half == 0 and position == 0:
                    value = value + straight
                outs[half][start : start + plan.rows, :] = value


def probs_kernel(q_hbm, k_hbm, error_ref, p_ref, own_ref, q_ref, k_ref, qsem, ksem):
    count, length = q_ref.shape[0], q_ref.shape[1]
    q_copy = lambda pair: pltpu.make_async_copy(q_hbm.at[pair], q_ref.at[pair], qsem.at[pair])
    k_copy = lambda pair: pltpu.make_async_copy(k_hbm.at[pair], k_ref.at[pair], ksem.at[pair])
    for pair in range(count):
        q_copy(pair).start()
        k_copy(pair).start()
    own_ref[...] = error_ref[...]

    group = group_of(count)

    def several(step, carry):
        for i in range(group):
            q_copy(step * group + i).wait()
            k_copy(step * group + i).wait()
        for i in range(group):
            pair = step * group + i
            key = k_ref[pair]
            for part in range(length // FCHUNK):
                rows = slice(part * FCHUNK, (part + 1) * FCHUNK)
                p_ref[pair, rows, :] = softmax_rows(q_ref[pair, rows, :], key)
        return carry

    lax.fori_loop(0, count // group, several, 0)


def backward_kernel(plan, dims, hw_hbm, head_hbm, p_ref, q_ref, k_ref, rsum_ref, *rest):
    layer_count, slot_count, heads = dims
    count = layer_count * slot_count
    pieces = plan.halves * plan.positions
    packed = rest[:pieces]
    qg_hbm, kg_hbm, wg_ref, hw_ref, head_ref, fmat, shift_ref, dmat, qg_ref, kg_ref, sems, qsem, ksem = rest[pieces:]
    length = q_ref.shape[1]
    scale = q_ref.shape[2] ** (-0.5)
    total = 2.0 * length
    q_copy = lambda pair: pltpu.make_async_copy(qg_ref.at[pair], qg_hbm.at[pair], qsem.at[pair])
    k_copy = lambda pair: pltpu.make_async_copy(kg_ref.at[pair], kg_hbm.at[pair], ksem.at[pair])
    head_copy = fetch(head_hbm, head_ref, sems.at[1])
    hw_copy = fetch(hw_hbm, hw_ref, sems.at[0])
    lanes = lax.broadcasted_iota(jnp.int32, (plan.extra, TILE), 1) if plan.folds else None
    diagonals = 0.0
    for half in range(plan.halves):
        for position in range(plan.positions):
            off = pl.multiple_of(plan.offset(half, position), 8)
            if plan.folds:
                ends = packed[half * plan.positions + position][len(plan.sent) * plan.rows : plan.size, :]
                diagonals = diagonals + jnp.where((lanes >= off) & (lanes < off + plan.rows), ends, 0.0)
            for at, (row, col) in enumerate(plan.sent):
                fmat[pl.ds(row * TILE + off, plan.rows), col * TILE : (col + 1) * TILE] = packed[
                    half * plan.positions + position
                ][at * plan.rows : (at + 1) * plan.rows, :]
    if plan.folds:
        upper, middle = triangle()
        for at, (high, low) in enumerate(plan.folds):
            hs, ls = slice(high * TILE, (high + 1) * TILE), slice(low * TILE, (low + 1) * TILE)
            both = fmat[hs, hs]
            turned = both.T
            fmat[hs, hs] = jnp.where(upper, both, turned)
            fmat[ls, ls] = jnp.where(middle, diagonals[at : at + 1, :], jnp.where(upper, turned, both))
    for row, col in plan.pairs:
        if row != col:
            rs, cs = slice(row * TILE, (row + 1) * TILE), slice(col * TILE, (col + 1) * TILE)
            fmat[cs, rs] = fmat[rs, cs].T
    shifts = jnp.dot(
        rsum_ref[...], fmat[...], precision=lax.Precision.HIGHEST, preferred_element_type=jnp.float32
    ) * (1.0 / total)
    shift_ref[...] = shifts
    head_copy.wait()
    hw_copy.wait()

    group = group_of(count)

    def several(step, carry):
        pairs = [step * group + i for i in range(group)]
        for i, pair in enumerate(pairs):
            weight = pair_weight(hw_ref, head_ref, pair, slot_count, heads)
            shift = shift_ref[pl.ds(pair, 1), :]
            rowsum = rsum_ref[pl.ds(pair, 1), :]
            tops = jnp.zeros((8, 1), jnp.float32)
            for part in range(length // BCHUNK):
                rows = slice(part * BCHUNK, (part + 1) * BCHUNK)
                probs = p_ref[pair, rows, :]
                raised = probs * (fmat[rows, :] - shift)
                rowtotal = jnp.sum(raised, axis=1, keepdims=True)
                tops = tops + jnp.sum(rowtotal.reshape(BCHUNK // 8, 8, 1), axis=0)
                dmat[i, rows, :] = (weight * (raised - probs * rowtotal)).astype(jnp.bfloat16)
            qgrad = jnp.dot(dmat[i], k_ref[pair], preferred_element_type=jnp.float32)
            qg_ref[pair] = (qgrad * scale).astype(jnp.bfloat16)
            kgrad = lax.dot_general(
                q_ref[pair], dmat[i], (((0,), (0,)), ((), ())), preferred_element_type=jnp.float32
            )
            kg_ref[pair] = (kgrad.T * scale).astype(jnp.bfloat16)
            grand = jnp.sum(shift * (0.5 * rowsum - 1.0), axis=1, keepdims=True) + jnp.sum(
                tops, axis=0, keepdims=True
            )
            wg_ref[pair // slot_count, pair % slot_count] = grand[0, 0]
            q_copy(pair).start()
            k_copy(pair).start()
        return carry

    lax.fori_loop(0, count // group, several, 0)
    for pair in range(count):
        q_copy(pair).wait()
        k_copy(pair).wait()


def swap(value, axis, size, flip):
    return lax.ppermute(value, axis, [(i, i ^ flip) for i in range(size)])


def across(value, layers, heads, layer_flip, head_flip):
    if layer_flip == 0:
        return swap(value, "head", heads, head_flip)
    if head_flip == 0:
        return swap(value, "layer", layers, layer_flip)
    pairs = [
        (la * heads + he, (la ^ layer_flip) * heads + (he ^ head_flip)) for la in range(layers) for he in range(heads)
    ]
    return lax.ppermute(value, ("layer", "head"), pairs)


def exchange_fast(plan, packed, probs_of):
    layers, heads, rows, blocks, size, share = plan.layers, plan.heads, plan.rows, plan.blocks, plan.size, plan.share
    chip = packed[0] + swap(packed[1], "head", heads, 1)
    got = []
    for position in range(1, plan.positions):
        value = chip[plan.start(position) : plan.start(position + 1)]
        got.append(across(value, layers, heads, position // 2, 2 * (position % 2)))
    tsym = chip[size : size + share] + got[0][size:]
    total = chip[:size]
    for value in got:
        total = total + value[:size]
    planes = {0: tsym}
    flip = blocks // 2
    while flip:
        order = sorted(planes)
        came = swap(jnp.concatenate([total] + [planes[i] for i in order], axis=0), "head", heads, 4 * flip)
        total = total + came[:size]
        for at, i in enumerate(order):
            planes[i ^ flip] = came[size + at * share : size + (at + 1) * share]
        flip = flip // 2
    plane = lax.axis_index("head") // 4

    def shared(row, col):
        value = planes[0]
        for flip in range(1, blocks):
            value = jnp.where((plane ^ flip) == row, planes[flip], value)
        return value[col * rows : (col + 1) * rows]

    off = plan.offset(0, 0)
    lows = dict(plan.folds)
    at_row = lax.broadcasted_iota(jnp.int32, (rows, TILE), 0) + off
    at_col = lax.broadcasted_iota(jnp.int32, (rows, TILE), 1)
    tparts = []
    for row, col in plan.sent:
        if row != col:
            tparts.append(shared(row, col) + shared(col, row))
        elif row in lows:
            tparts.append(jnp.where(at_col >= at_row, shared(row, row), shared(lows[row], lows[row])))
        else:
            tparts.append(shared(row, row))
    if plan.folds:
        ends = [jnp.sum(jnp.where(at_col == at_row, shared(low, low), 0.0), axis=0, keepdims=True) for _, low in plan.folds]
        tparts.append(jnp.pad(jnp.concatenate(ends, axis=0), ((0, plan.extra - len(ends)), (0, 0))))
    error = 2.0 * jax.nn.sigmoid(total) - jnp.concatenate(tparts, axis=0)
    parts = []
    for position in range(1, plan.positions):
        parts.append(across(error, layers, heads, position // 2, 2 * (position % 2)))
    probs, error, *vectors = probs_of(error)
    mine = [error] + parts
    return [probs] + vectors, mine + [swap(part, "head", heads, 1) for part in mine]


def exchange_general(plan, packed, target, probs_of):
    logit = lax.psum(packed[0], ("layer", "head"))
    whole = lax.all_gather(target, "head", axis=0, tiled=True)
    whole = (whole + whole.T).astype(jnp.float32)
    parts = [whole[r * TILE : (r + 1) * TILE, c * TILE : (c + 1) * TILE] for r, c in plan.pairs]
    probs, error, *vectors = probs_of(2.0 * jax.nn.sigmoid(logit) - jnp.concatenate(parts, axis=0))
    return [probs] + vectors, [error]


def on_device(layers, heads_axis, queries, keys, head_weight, slot_head, target):
    layer_count, slot_count, length, size = queries.shape
    heads = head_weight.shape[1]
    count = layer_count * slot_count
    plan = Plan(layers, heads_axis, length)
    flat_q = queries.reshape(count, length, size)
    flat_k = keys.reshape(count, length, size)
    dims = (layer_count, slot_count, heads)
    hbm = pl.BlockSpec(memory_space=pltpu.HBM)
    vmem = pl.BlockSpec(memory_space=pltpu.VMEM)
    smem = pl.BlockSpec(memory_space=pltpu.SMEM)
    sums_shape = (pad8(count), length)
    params = pltpu.CompilerParams(vmem_limit_bytes=12 * 2**20)
    weights = [pltpu.SMEM(head_weight.shape, jnp.float32), pltpu.SMEM(slot_head.shape, jnp.int32)]
    pair_sems = pltpu.SemaphoreType.DMA((count,))
    head_weight, target_hbm, first_q, first_k = (
        pltpu.with_memory_space_constraint(value, pltpu.HBM) for value in (head_weight, target, flat_q, flat_k)
    )
    if slot_count > 1:
        slot_head = pltpu.with_memory_space_constraint(slot_head, pltpu.HBM)
    fwd = pl.pallas_call(
        functools.partial(forward_kernel, plan, dims),
        in_specs=[hbm] * 5,
        out_specs=[vmem] * (plan.halves + 1),
        out_shape=[pltpu.VMEM((plan.start(plan.positions), TILE), jnp.float32)] * plan.halves
        + [pltpu.VMEM(sums_shape, jnp.float32)],
        scratch_shapes=weights
        + [
            pltpu.VMEM(target.shape, jnp.int32),
            pltpu.VMEM(flat_q.shape, jnp.bfloat16),
            pltpu.VMEM(flat_q.shape, jnp.bfloat16),
            pltpu.VMEM((length, length), jnp.float32),
            pltpu.VMEM(sums_shape, jnp.float32),
            pltpu.VMEM((TILE, length), jnp.float32),
            pltpu.SemaphoreType.DMA((3,)),
            pair_sems,
            pair_sems,
        ],
        compiler_params=params,
        name="forward_maps",
    )(head_weight, slot_head, target_hbm, first_q, first_k)
    packed, rsum = fwd[: plan.halves], fwd[plan.halves]

    def probs_of(error):
        return pl.pallas_call(
            probs_kernel,
            in_specs=[hbm, hbm, vmem],
            out_specs=[vmem] * 4,
            out_shape=[
                pltpu.VMEM((count, length, length), jnp.float32),
                pltpu.VMEM(error.shape, jnp.float32),
                pltpu.VMEM(flat_q.shape, jnp.bfloat16),
                pltpu.VMEM(flat_q.shape, jnp.bfloat16),
            ],
            scratch_shapes=[pair_sems, pair_sems],
            compiler_params=params,
            cost_estimate=pl.CostEstimate(
                flops=2 * count * length * length * size,
                bytes_accessed=4 * count * length * length,
                transcendentals=count * length * length,
            ),
            name="probs_maps",
        )(first_q, first_k, error)

    if plan.fast:
        held, errors = exchange_fast(plan, packed, probs_of)
    else:
        held, errors = exchange_general(plan, packed, target, probs_of)
    qgrad, kgrad, wgrad = pl.pallas_call(
        functools.partial(backward_kernel, plan, dims),
        in_specs=[hbm] * 2 + [vmem] * (4 + plan.halves * plan.positions),
        out_specs=[hbm, hbm, smem],
        out_shape=[
            pltpu.HBM((count, length, size), jnp.bfloat16),
            pltpu.HBM((count, length, size), jnp.bfloat16),
            jax.ShapeDtypeStruct((layer_count, slot_count), jnp.float32),
        ],
        scratch_shapes=weights
        + [
            pltpu.VMEM((length, length), jnp.float32),
            pltpu.VMEM(sums_shape, jnp.float32),
            pltpu.VMEM((group_of(count), length, length), jnp.bfloat16),
            pltpu.VMEM(flat_q.shape, jnp.bfloat16),
            pltpu.VMEM(flat_q.shape, jnp.bfloat16),
            pltpu.SemaphoreType.DMA((2,)),
            pair_sems,
            pair_sems,
        ],
        compiler_params=params,
        name="backward_maps",
    )(head_weight, slot_head, *held, rsum, *errors)
    return qgrad.reshape(queries.shape), kgrad.reshape(queries.shape), wgrad


def solution(mesh):
    return jax.shard_map(
        functools.partial(on_device, mesh.shape["layer"], mesh.shape["head"]),
        mesh=mesh,
        in_specs=(
            P("layer", "head", None, None),
            P("layer", "head", None, None),
            P("layer", None),
            P("head"),
            P("head", None),
        ),
        out_specs=(
            P("layer", "head", None, None),
            P("layer", "head", None, None),
            P("layer", "head"),
        ),
        check_vma=False,
    )
```

```python
import functools

import jax
import jax.numpy as jnp
from jax import lax
from jax.experimental import pallas as pl
from jax.experimental.pallas import tpu as pltpu
from jax.sharding import PartitionSpec as P

TILE = 128
LOG2E = 1.4426950408889634
FCHUNK = 256
BCHUNK = 256


def block_pairs(count):
    pairs = []
    for row in range(count):
        for col in range(count):
            gap = (col - row) % count
            if 2 * gap < count or (2 * gap == count and row < col):
                pairs.append((row, col))
    return pairs


def group_of(count):
    return 3 if count % 3 == 0 else 2 if count % 2 == 0 else 1


def pad8(count):
    return -(-count // 8) * 8


def split3(value):
    first = value.astype(jnp.bfloat16).astype(jnp.float32)
    rest = value - first
    second = rest.astype(jnp.bfloat16).astype(jnp.float32)
    return first, second, rest - second


def pair_weight(hw_ref, head_ref, pair, slot_count, heads):
    layer, slot = pair // slot_count, pair % slot_count
    held = head_ref[slot]
    return jnp.where(held < heads, hw_ref[layer, jnp.minimum(held, heads - 1)], 0.0)


class Plan:
    def __init__(self, layers, heads, length):
        self.blocks = length // TILE
        self.pairs = block_pairs(self.blocks)
        self.layers, self.heads = layers, heads
        self.fast = (
            heads % 4 == 0
            and heads // 4 == self.blocks
            and self.blocks & (self.blocks - 1) == 0
            and layers & (layers - 1) == 0
            and (TILE // (4 * layers)) % 8 == 0
        )
        self.halves = 2 if self.fast else 1
        self.positions = 2 * layers if self.fast else 1
        self.rows = TILE // (self.halves * self.positions)
        self.folds = [(i, i + 1) for i in range(0, self.blocks, 2)] if self.fast and self.blocks % 2 == 0 else []
        lower = [low for _, low in self.folds]
        self.sent = [(row, col) for row, col in self.pairs if row != col or row not in lower]
        self.extra = pad8(len(self.folds))
        self.size = len(self.sent) * self.rows + self.extra
        self.share = self.blocks * self.rows if self.fast else 0

    def start(self, position):
        return position * self.size + min(position, 1) * self.share + (self.share // 2 if position > 1 else 0)

    def offset(self, half, position):
        if not self.fast:
            return 0
        head = lax.axis_index("head")
        core = (head % 2) ^ half
        y_at = ((head // 2) % 2) ^ (position % 2)
        layer = lax.axis_index("layer") ^ (position // 2)
        return ((2 * y_at + core) * self.layers + layer) * self.rows


def triangle():
    rows = lax.broadcasted_iota(jnp.int32, (TILE, TILE), 0)
    cols = lax.broadcasted_iota(jnp.int32, (TILE, TILE), 1)
    return cols >= rows, cols == rows


def fetch(source, target, sem):
    copy = pltpu.make_async_copy(source, target, sem)
    copy.start()
    return copy


def softmax_rows(query, key):
    scores = lax.dot_general(query, key, (((1,), (1,)), ((), ())), preferred_element_type=jnp.float32)
    highest = jnp.max(scores, axis=1, keepdims=True)
    expo = jnp.exp2((scores - highest) * (LOG2E * query.shape[-1] ** (-0.5)))
    return expo * (1.0 / jnp.sum(expo, axis=1, keepdims=True))


def forward_kernel(plan, dims, hw_hbm, head_hbm, t_hbm, q_hbm, k_hbm, *rest):
    layer_count, slot_count, heads = dims
    count = layer_count * slot_count
    outs, rsum_ref = rest[: plan.halves], rest[plan.halves]
    hw_ref, head_ref, t_ref, q_ref, k_ref, acc, scaled, flip, sems, qsem, ksem = rest[plan.halves + 1 :]
    length = q_ref.shape[1]
    total = 2.0 * length
    group = group_of(count)
    q_copy = lambda step: pltpu.make_async_copy(
        q_hbm.at[pl.ds(step * group, group)], q_ref.at[pl.ds(step * group, group)], qsem.at[step]
    )
    k_copy = lambda step: pltpu.make_async_copy(
        k_hbm.at[pl.ds(step * group, group)], k_ref.at[pl.ds(step * group, group)], ksem.at[step]
    )
    t_copy = fetch(t_hbm, t_ref, sems.at[2])
    for step in range(count // group):
        q_copy(step).start()
        k_copy(step).start()
        if step == 0:
            head_copy = fetch(head_hbm, head_ref, sems.at[1])
            hw_copy = fetch(hw_hbm, hw_ref, sems.at[0])
    acc[...] = jnp.zeros_like(acc)
    scaled[...] = jnp.zeros_like(scaled)
    rsum_ref[...] = jnp.zeros_like(rsum_ref)
    if plan.fast:
        target_share(plan, t_ref, t_copy, flip, outs)
    else:
        t_copy.wait()
    head_copy.wait()
    hw_copy.wait()

    def several(step, carry):
        pairs = [step * group + i for i in range(group)]
        q_copy(step).wait()
        k_copy(step).wait()
        weights = [pair_weight(hw_ref, head_ref, pair, slot_count, heads) for pair in pairs]
        colsums = [jnp.zeros((8, length), jnp.float32) for _ in pairs]
        for part in range(length // FCHUNK):
            rows = slice(part * FCHUNK, (part + 1) * FCHUNK)
            added = acc[rows, :]
            for i, pair in enumerate(pairs):
                probs = softmax_rows(q_ref[pair, rows, :], k_ref[pair])
                added = added + weights[i] * probs
                colsums[i] = colsums[i] + jnp.sum(probs.reshape(FCHUNK // 8, 8, length), axis=0)
            acc[rows, :] = added
        for i, pair in enumerate(pairs):
            rowsum = 1.0 + jnp.sum(colsums[i], axis=0, keepdims=True)
            rsum_ref[pl.ds(pair, 1), :] = rowsum
            scaled[pl.ds(pair, 1), :] = rowsum * (-weights[i] / total)
        return carry

    lax.fori_loop(0, count // group, several, 0)
    left = split3(scaled[...])
    right = split3(rsum_ref[...])
    order = ((0, 0), (0, 1), (1, 0), (1, 1), (0, 2), (2, 0))
    lefts = jnp.concatenate([left[a] for a, _ in order], axis=0).astype(jnp.bfloat16)
    rights = jnp.concatenate([right[b] for _, b in order], axis=0).astype(jnp.bfloat16)
    for row, col in plan.pairs:
        rs, cs = slice(row * TILE, (row + 1) * TILE), slice(col * TILE, (col + 1) * TILE)
        both = acc[rs, cs] + acc[cs, rs].T
        acc[rs, cs] = both + lax.dot_general(
            lefts[:, rs], rights[:, cs], (((0,), (0,)), ((), ())), preferred_element_type=jnp.float32
        )
    diagonals = []
    if plan.folds:
        upper, middle = triangle()
        for high, low in plan.folds:
            hs, ls = slice(high * TILE, (high + 1) * TILE), slice(low * TILE, (low + 1) * TILE)
            below = acc[ls, ls]
            acc[hs, hs] = jnp.where(upper, acc[hs, hs], below)
            diagonals.append(jnp.sum(jnp.where(middle, below, 0.0), axis=0, keepdims=True))
        diagonals.append(jnp.zeros((plan.extra - len(plan.folds), TILE), jnp.float32))
        diagonals = jnp.concatenate(diagonals, axis=0)
    for half in range(plan.halves):
        for position in range(plan.positions):
            off = pl.multiple_of(plan.offset(half, position), 8)
            for at, (row, col) in enumerate(plan.sent):
                start = plan.start(position) + at * plan.rows
                outs[half][start : start + plan.rows, :] = acc[
                    pl.ds(row * TILE + off, plan.rows), col * TILE : (col + 1) * TILE
                ]
            if plan.folds:
                start = plan.start(position) + len(plan.sent) * plan.rows
                outs[half][start : start + plan.extra, :] = diagonals


def target_share(plan, t_ref, t_copy, flip, outs):
    head = lax.axis_index("head")
    core, y_at, plane = head % 2, (head // 2) % 2, head // 4
    strip = TILE // 4
    flip[...] = jnp.zeros_like(flip)
    t_copy.wait()
    flip[pl.ds(pl.multiple_of(strip * (2 * y_at + core), 8), strip), :] = t_ref[...].astype(jnp.float32)
    natural = pl.multiple_of(plan.offset(0, 0), 8)
    for col in range(plan.blocks):
        gap = (col - plane + plan.blocks) % plan.blocks
        is_natural = (2 * gap < plan.blocks) | ((2 * gap == plan.blocks) & (plane < col))
        keep_natural = jnp.where(is_natural, 1.0, 0.0)
        keep_flipped = jnp.where(is_natural & (gap != 0), 0.0, 1.0)
        cols = slice(col * TILE, (col + 1) * TILE)
        straight = flip[pl.ds(natural, plan.rows), cols] * keep_natural
        turned = (flip[:, cols] * keep_flipped).T
        flip[:, cols] = turned
        for half in range(plan.halves):
            off = pl.multiple_of(plan.offset(half, 0), 8)
            start = plan.size + col * plan.rows
            value = flip[pl.ds(off, plan.rows), cols]
            outs[half][start : start + plan.rows, :] = value + straight if half == 0 else value
            if col % 2 == 0:
                continue
            off = pl.multiple_of(plan.offset(half, 1), 8)
            start = plan.start(1) + plan.size + col // 2 * plan.rows
            before = flip[pl.ds(off, plan.rows), (col - 1) * TILE : col * TILE]
            outs[half][start : start + plan.rows, :] = before + pltpu.roll(
                flip[pl.ds(off, plan.rows), cols], TILE // 2, 1
            )


def probs_kernel(q_hbm, k_hbm, error_ref, p_ref, own_ref, q_ref, k_ref, qsem, ksem):
    count, length = q_ref.shape[0], q_ref.shape[1]
    group = group_of(count)
    q_copy = lambda step: pltpu.make_async_copy(
        q_hbm.at[pl.ds(step * group, group)], q_ref.at[pl.ds(step * group, group)], qsem.at[step]
    )
    k_copy = lambda step: pltpu.make_async_copy(
        k_hbm.at[pl.ds(step * group, group)], k_ref.at[pl.ds(step * group, group)], ksem.at[step]
    )
    for step in range(count // group):
        q_copy(step).start()
        k_copy(step).start()
    own_ref[...] = error_ref[...]


    def several(step, carry):
        q_copy(step).wait()
        k_copy(step).wait()
        for i in range(group):
            pair = step * group + i
            key = k_ref[pair]
            for part in range(length // FCHUNK):
                rows = slice(part * FCHUNK, (part + 1) * FCHUNK)
                p_ref[pair, rows, :] = softmax_rows(q_ref[pair, rows, :], key)
        return carry

    lax.fori_loop(0, count // group, several, 0)


def backward_kernel(plan, dims, hw_hbm, head_hbm, p_ref, q_ref, k_ref, rsum_ref, *rest):
    layer_count, slot_count, heads = dims
    count = layer_count * slot_count
    pieces = plan.halves * plan.positions
    packed = rest[:pieces]
    qg_hbm, kg_hbm, wg_ref, hw_ref, head_ref, fmat, shift_ref, dmat, qg_ref, kg_ref, sems, qsem, ksem = rest[pieces:]
    length = q_ref.shape[1]
    scale = q_ref.shape[2] ** (-0.5)
    total = 2.0 * length
    q_copy = lambda pair: pltpu.make_async_copy(qg_ref.at[pair], qg_hbm.at[pair], qsem.at[pair])
    k_copy = lambda pair: pltpu.make_async_copy(kg_ref.at[pair], kg_hbm.at[pair], ksem.at[pair])
    head_copy = fetch(head_hbm, head_ref, sems.at[1])
    hw_copy = fetch(hw_hbm, hw_ref, sems.at[0])
    lanes = lax.broadcasted_iota(jnp.int32, (plan.extra, TILE), 1) if plan.folds else None
    diagonals = 0.0
    for half in range(plan.halves):
        for position in range(plan.positions):
            off = pl.multiple_of(plan.offset(half, position), 8)
            if plan.folds:
                ends = packed[half * plan.positions + position][len(plan.sent) * plan.rows : plan.size, :]
                diagonals = diagonals + jnp.where((lanes >= off) & (lanes < off + plan.rows), ends, 0.0)
            for at, (row, col) in enumerate(plan.sent):
                fmat[pl.ds(row * TILE + off, plan.rows), col * TILE : (col + 1) * TILE] = packed[
                    half * plan.positions + position
                ][at * plan.rows : (at + 1) * plan.rows, :]
    if plan.folds:
        upper, middle = triangle()
        for at, (high, low) in enumerate(plan.folds):
            hs, ls = slice(high * TILE, (high + 1) * TILE), slice(low * TILE, (low + 1) * TILE)
            both = fmat[hs, hs]
            turned = both.T
            fmat[hs, hs] = jnp.where(upper, both, turned)
            fmat[ls, ls] = jnp.where(middle, diagonals[at : at + 1, :], jnp.where(upper, turned, both))
    for row, col in plan.pairs:
        if row != col:
            rs, cs = slice(row * TILE, (row + 1) * TILE), slice(col * TILE, (col + 1) * TILE)
            fmat[cs, rs] = fmat[rs, cs].T
    shifts = jnp.dot(
        rsum_ref[...], fmat[...], precision=lax.Precision.HIGHEST, preferred_element_type=jnp.float32
    ) * (1.0 / total)
    shift_ref[...] = shifts
    head_copy.wait()
    hw_copy.wait()

    group = group_of(count)

    def several(step, carry):
        pairs = [step * group + i for i in range(group)]
        for i, pair in enumerate(pairs):
            weight = pair_weight(hw_ref, head_ref, pair, slot_count, heads)
            shift = shift_ref[pl.ds(pair, 1), :]
            rowsum = rsum_ref[pl.ds(pair, 1), :]
            tops = jnp.zeros((8, 1), jnp.float32)
            for part in range(length // BCHUNK):
                rows = slice(part * BCHUNK, (part + 1) * BCHUNK)
                probs = p_ref[pair, rows, :]
                raised = probs * (fmat[rows, :] - shift)
                rowtotal = jnp.sum(raised, axis=1, keepdims=True)
                tops = tops + jnp.sum(rowtotal.reshape(BCHUNK // 8, 8, 1), axis=0)
                dmat[i, rows, :] = (weight * (raised - probs * rowtotal)).astype(jnp.bfloat16)
            qgrad = jnp.dot(dmat[i], k_ref[pair], preferred_element_type=jnp.float32)
            qg_ref[pair] = (qgrad * scale).astype(jnp.bfloat16)
            kgrad = lax.dot_general(
                q_ref[pair], dmat[i], (((0,), (0,)), ((), ())), preferred_element_type=jnp.float32
            )
            kg_ref[pair] = (kgrad.T * scale).astype(jnp.bfloat16)
            grand = jnp.sum(shift * (0.5 * rowsum - 1.0), axis=1, keepdims=True) + jnp.sum(
                tops, axis=0, keepdims=True
            )
            wg_ref[pair // slot_count, pair % slot_count] = grand[0, 0]
            q_copy(pair).start()
            k_copy(pair).start()
        return carry

    lax.fori_loop(0, count // group, several, 0)
    for pair in range(count):
        q_copy(pair).wait()
        k_copy(pair).wait()


def swap(value, axis, size, flip):
    return lax.ppermute(value, axis, [(i, i ^ flip) for i in range(size)])


def across(value, layers, heads, layer_flip, head_flip):
    if layer_flip == 0:
        return swap(value, "head", heads, head_flip)
    if head_flip == 0:
        return swap(value, "layer", layers, layer_flip)
    pairs = [
        (la * heads + he, (la ^ layer_flip) * heads + (he ^ head_flip)) for la in range(layers) for he in range(heads)
    ]
    return lax.ppermute(value, ("layer", "head"), pairs)


def exchange_fast(plan, packed, probs_of):
    layers, heads, rows, blocks, size, share = plan.layers, plan.heads, plan.rows, plan.blocks, plan.size, plan.share
    chip = packed[0] + swap(packed[1], "head", heads, 1)
    got = []
    for position in range(1, plan.positions):
        value = chip[plan.start(position) : plan.start(position + 1)]
        got.append(across(value, layers, heads, position // 2, 2 * (position % 2)))
    y_at = (lax.axis_index("head") // 2) % 2
    theirs = lax.broadcasted_iota(jnp.int32, (share // 2, TILE), 1) // (TILE // 2) != y_at
    came = got[0][size:]
    evens = jnp.where(theirs, came, 0.0)
    odds = jnp.where(theirs, jnp.concatenate([came[:, TILE // 2 :], came[:, : TILE // 2]], axis=1), 0.0)
    parts = [half[at * rows : (at + 1) * rows] for at in range(blocks // 2) for half in (evens, odds)]
    tsym = chip[size : size + share] + jnp.concatenate(parts, axis=0)
    total = chip[:size]
    for value in got:
        total = total + value[:size]
    planes = {0: tsym}
    flip = blocks // 2
    while flip:
        order = sorted(planes)
        came = swap(jnp.concatenate([total] + [planes[i] for i in order], axis=0), "head", heads, 4 * flip)
        total = total + came[:size]
        for at, i in enumerate(order):
            planes[i ^ flip] = came[size + at * share : size + (at + 1) * share]
        flip = flip // 2
    plane = lax.axis_index("head") // 4

    def shared(row, col):
        value = planes[0]
        for flip in range(1, blocks):
            value = jnp.where((plane ^ flip) == row, planes[flip], value)
        return value[col * rows : (col + 1) * rows]

    off = plan.offset(0, 0)
    lows = dict(plan.folds)
    at_row = lax.broadcasted_iota(jnp.int32, (rows, TILE), 0) + off
    at_col = lax.broadcasted_iota(jnp.int32, (rows, TILE), 1)
    tparts = []
    for row, col in plan.sent:
        if row != col:
            tparts.append(shared(row, col) + shared(col, row))
        elif row in lows:
            tparts.append(jnp.where(at_col >= at_row, shared(row, row), shared(lows[row], lows[row])))
        else:
            tparts.append(shared(row, row))
    if plan.folds:
        ends = [jnp.sum(jnp.where(at_col == at_row, shared(low, low), 0.0), axis=0, keepdims=True) for _, low in plan.folds]
        tparts.append(jnp.pad(jnp.concatenate(ends, axis=0), ((0, plan.extra - len(ends)), (0, 0))))
    error = 2.0 * jax.nn.sigmoid(total) - jnp.concatenate(tparts, axis=0)
    parts = []
    for position in range(1, plan.positions):
        parts.append(across(error, layers, heads, position // 2, 2 * (position % 2)))
    probs, error, *vectors = probs_of(error)
    mine = [error] + parts
    return [probs] + vectors, mine + [swap(part, "head", heads, 1) for part in mine]


def exchange_general(plan, packed, target, probs_of):
    logit = lax.psum(packed[0], ("layer", "head"))
    whole = lax.all_gather(target, "head", axis=0, tiled=True)
    whole = (whole + whole.T).astype(jnp.float32)
    parts = [whole[r * TILE : (r + 1) * TILE, c * TILE : (c + 1) * TILE] for r, c in plan.pairs]
    probs, error, *vectors = probs_of(2.0 * jax.nn.sigmoid(logit) - jnp.concatenate(parts, axis=0))
    return [probs] + vectors, [error]


def on_device(layers, heads_axis, queries, keys, head_weight, slot_head, target):
    layer_count, slot_count, length, size = queries.shape
    heads = head_weight.shape[1]
    count = layer_count * slot_count
    plan = Plan(layers, heads_axis, length)
    flat_q = queries.reshape(count, length, size)
    flat_k = keys.reshape(count, length, size)
    dims = (layer_count, slot_count, heads)
    hbm = pl.BlockSpec(memory_space=pltpu.HBM)
    vmem = pl.BlockSpec(memory_space=pltpu.VMEM)
    smem = pl.BlockSpec(memory_space=pltpu.SMEM)
    sums_shape = (pad8(count), length)
    params = pltpu.CompilerParams(vmem_limit_bytes=12 * 2**20)
    weights = [pltpu.SMEM(head_weight.shape, jnp.float32), pltpu.SMEM(slot_head.shape, jnp.int32)]
    pair_sems = pltpu.SemaphoreType.DMA((count,))
    head_weight, target_hbm, first_q, first_k = (
        pltpu.with_memory_space_constraint(value, pltpu.HBM) for value in (head_weight, target, flat_q, flat_k)
    )
    if slot_count > 1:
        slot_head = pltpu.with_memory_space_constraint(slot_head, pltpu.HBM)
    fwd = pl.pallas_call(
        functools.partial(forward_kernel, plan, dims),
        in_specs=[hbm] * 5,
        out_specs=[vmem] * (plan.halves + 1),
        out_shape=[pltpu.VMEM((plan.start(plan.positions), TILE), jnp.float32)] * plan.halves
        + [pltpu.VMEM(sums_shape, jnp.float32)],
        scratch_shapes=weights
        + [
            pltpu.VMEM(target.shape, jnp.int32),
            pltpu.VMEM(flat_q.shape, jnp.bfloat16),
            pltpu.VMEM(flat_q.shape, jnp.bfloat16),
            pltpu.VMEM((length, length), jnp.float32),
            pltpu.VMEM(sums_shape, jnp.float32),
            pltpu.VMEM((TILE, length), jnp.float32),
            pltpu.SemaphoreType.DMA((3,)),
            pair_sems,
            pair_sems,
        ],
        compiler_params=params,
        name="forward_maps",
    )(head_weight, slot_head, target_hbm, first_q, first_k)
    packed, rsum = fwd[: plan.halves], fwd[plan.halves]

    def probs_of(error):
        return pl.pallas_call(
            probs_kernel,
            in_specs=[hbm, hbm, vmem],
            out_specs=[vmem] * 4,
            out_shape=[
                pltpu.VMEM((count, length, length), jnp.float32),
                pltpu.VMEM(error.shape, jnp.float32),
                pltpu.VMEM(flat_q.shape, jnp.bfloat16),
                pltpu.VMEM(flat_q.shape, jnp.bfloat16),
            ],
            scratch_shapes=[pair_sems, pair_sems],
            compiler_params=params,
            cost_estimate=pl.CostEstimate(
                flops=2 * count * length * length * size,
                bytes_accessed=4 * count * length * length,
                transcendentals=count * length * length,
            ),
            name="probs_maps",
        )(first_q, first_k, error)

    if plan.fast:
        held, errors = exchange_fast(plan, packed, probs_of)
    else:
        held, errors = exchange_general(plan, packed, target, probs_of)
    qgrad, kgrad, wgrad = pl.pallas_call(
        functools.partial(backward_kernel, plan, dims),
        in_specs=[hbm] * 2 + [vmem] * (4 + plan.halves * plan.positions),
        out_specs=[hbm, hbm, smem],
        out_shape=[
            pltpu.HBM((count, length, size), jnp.bfloat16),
            pltpu.HBM((count, length, size), jnp.bfloat16),
            jax.ShapeDtypeStruct((layer_count, slot_count), jnp.float32),
        ],
        scratch_shapes=weights
        + [
            pltpu.VMEM((length, length), jnp.float32),
            pltpu.VMEM(sums_shape, jnp.float32),
            pltpu.VMEM((group_of(count), length, length), jnp.bfloat16),
            pltpu.VMEM(flat_q.shape, jnp.bfloat16),
            pltpu.VMEM(flat_q.shape, jnp.bfloat16),
            pltpu.SemaphoreType.DMA((2,)),
            pair_sems,
            pair_sems,
        ],
        compiler_params=params,
        name="backward_maps",
    )(head_weight, slot_head, *held, rsum, *errors)
    return qgrad.reshape(queries.shape), kgrad.reshape(queries.shape), wgrad


def solution(mesh):
    return jax.shard_map(
        functools.partial(on_device, mesh.shape["layer"], mesh.shape["head"]),
        mesh=mesh,
        in_specs=(
            P("layer", "head", None, None),
            P("layer", "head", None, None),
            P("layer", None),
            P("head"),
            P("head", None),
        ),
        out_specs=(
            P("layer", "head", None, None),
            P("layer", "head", None, None),
            P("layer", "head"),
        ),
        check_vma=False,
    )
```

```python
import functools

import jax
import jax.numpy as jnp
from jax import lax
from jax.experimental import pallas as pl
from jax.experimental.pallas import tpu as pltpu
from jax.sharding import PartitionSpec as P

TILE = 128
LOG2E = 1.4426950408889634
FCHUNK = 256
BCHUNK = 256


def block_pairs(count):
    pairs = []
    for row in range(count):
        for col in range(count):
            gap = (col - row) % count
            if 2 * gap < count or (2 * gap == count and row < col):
                pairs.append((row, col))
    return pairs


def group_of(count):
    return 3 if count % 3 == 0 else 2 if count % 2 == 0 else 1


def pad8(count):
    return -(-count // 8) * 8


def split3(value):
    first = value.astype(jnp.bfloat16).astype(jnp.float32)
    rest = value - first
    second = rest.astype(jnp.bfloat16).astype(jnp.float32)
    return first, second, rest - second


def pair_weight(hw_ref, head_ref, pair, slot_count, heads):
    layer, slot = pair // slot_count, pair % slot_count
    held = head_ref[slot]
    return jnp.where(held < heads, hw_ref[layer, jnp.minimum(held, heads - 1)], 0.0)


class Plan:
    def __init__(self, layers, heads, length):
        self.blocks = length // TILE
        self.pairs = block_pairs(self.blocks)
        self.layers, self.heads = layers, heads
        self.fast = (
            heads % 4 == 0
            and heads // 4 == self.blocks
            and self.blocks & (self.blocks - 1) == 0
            and layers & (layers - 1) == 0
            and (TILE // (4 * layers)) % 8 == 0
        )
        self.halves = 2 if self.fast else 1
        self.positions = 2 * layers if self.fast else 1
        self.rows = TILE // (self.halves * self.positions)
        self.folds = [(i, i + 1) for i in range(0, self.blocks, 2)] if self.fast and self.blocks % 2 == 0 else []
        lower = [low for _, low in self.folds]
        self.sent = [(row, col) for row, col in self.pairs if row != col or row not in lower]
        self.extra = pad8(len(self.folds))
        self.size = len(self.sent) * self.rows + self.extra
        self.share = self.blocks * self.rows if self.fast else 0

    def start(self, position):
        return position * self.size + min(position, 1) * self.share + (self.share // 2 if position > 1 else 0)

    def offset(self, half, position):
        if not self.fast:
            return 0
        head = lax.axis_index("head")
        core = (head % 2) ^ half
        y_at = ((head // 2) % 2) ^ (position % 2)
        layer = lax.axis_index("layer") ^ (position // 2)
        return ((2 * y_at + core) * self.layers + layer) * self.rows


def triangle():
    rows = lax.broadcasted_iota(jnp.int32, (TILE, TILE), 0)
    cols = lax.broadcasted_iota(jnp.int32, (TILE, TILE), 1)
    return cols >= rows, cols == rows


def fetch(source, target, sem):
    copy = pltpu.make_async_copy(source, target, sem)
    copy.start()
    return copy


def softmax_rows(query, key):
    scores = lax.dot_general(query, key, (((1,), (1,)), ((), ())), preferred_element_type=jnp.float32)
    highest = jnp.max(scores, axis=1, keepdims=True)
    expo = jnp.exp2((scores - highest) * (LOG2E * query.shape[-1] ** (-0.5)))
    return expo * (1.0 / jnp.sum(expo, axis=1, keepdims=True))


def forward_kernel(plan, dims, hw_hbm, head_hbm, t_hbm, q_hbm, k_hbm, *rest):
    layer_count, slot_count, heads = dims
    count = layer_count * slot_count
    outs, rsum_ref = rest[: plan.halves], rest[plan.halves]
    hw_ref, head_ref, t_ref, q_ref, k_ref, acc, scaled, flip, sems, qsem, ksem = rest[plan.halves + 1 :]
    length = q_ref.shape[1]
    total = 2.0 * length
    group = group_of(count)
    q_copy = lambda step: pltpu.make_async_copy(
        q_hbm.at[pl.ds(step * group, group)], q_ref.at[pl.ds(step * group, group)], qsem.at[step]
    )
    k_copy = lambda step: pltpu.make_async_copy(
        k_hbm.at[pl.ds(step * group, group)], k_ref.at[pl.ds(step * group, group)], ksem.at[step]
    )
    t_copy = fetch(t_hbm, t_ref, sems.at[2])
    for step in range(count // group):
        q_copy(step).start()
        k_copy(step).start()
        if step == 0:
            head_copy = fetch(head_hbm, head_ref, sems.at[1])
            hw_copy = fetch(hw_hbm, hw_ref, sems.at[0])
    acc[...] = jnp.zeros_like(acc)
    scaled[...] = jnp.zeros_like(scaled)
    rsum_ref[...] = jnp.zeros_like(rsum_ref)
    if plan.fast:
        target_share(plan, t_ref, t_copy, flip, outs)
    else:
        t_copy.wait()
    head_copy.wait()
    hw_copy.wait()

    def several(step, carry):
        pairs = [step * group + i for i in range(group)]
        q_copy(step).wait()
        k_copy(step).wait()
        weights = [pair_weight(hw_ref, head_ref, pair, slot_count, heads) for pair in pairs]
        colsums = [jnp.zeros((8, length), jnp.float32) for _ in pairs]
        for part in range(length // FCHUNK):
            rows = slice(part * FCHUNK, (part + 1) * FCHUNK)
            added = acc[rows, :]
            for i, pair in enumerate(pairs):
                probs = softmax_rows(q_ref[pair, rows, :], k_ref[pair])
                added = added + weights[i] * probs
                colsums[i] = colsums[i] + jnp.sum(probs.reshape(FCHUNK // 8, 8, length), axis=0)
            acc[rows, :] = added
        for i, pair in enumerate(pairs):
            rowsum = 1.0 + jnp.sum(colsums[i], axis=0, keepdims=True)
            rsum_ref[pl.ds(pair, 1), :] = rowsum
            scaled[pl.ds(pair, 1), :] = rowsum * (-weights[i] / total)
        return carry

    lax.fori_loop(0, count // group, several, 0)
    left = split3(scaled[...])
    right = split3(rsum_ref[...])
    order = ((0, 0), (0, 1), (1, 0), (1, 1), (0, 2), (2, 0))
    lefts = jnp.concatenate([left[a] for a, _ in order], axis=0).astype(jnp.bfloat16)
    rights = jnp.concatenate([right[b] for _, b in order], axis=0).astype(jnp.bfloat16)
    for row, col in plan.pairs:
        rs, cs = slice(row * TILE, (row + 1) * TILE), slice(col * TILE, (col + 1) * TILE)
        both = acc[rs, cs] + acc[cs, rs].T
        acc[rs, cs] = both + lax.dot_general(
            lefts[:, rs], rights[:, cs], (((0,), (0,)), ((), ())), preferred_element_type=jnp.float32
        )
    diagonals = []
    if plan.folds:
        upper, middle = triangle()
        for high, low in plan.folds:
            hs, ls = slice(high * TILE, (high + 1) * TILE), slice(low * TILE, (low + 1) * TILE)
            below = acc[ls, ls]
            acc[hs, hs] = jnp.where(upper, acc[hs, hs], below)
            diagonals.append(jnp.sum(jnp.where(middle, below, 0.0), axis=0, keepdims=True))
        diagonals.append(jnp.zeros((plan.extra - len(plan.folds), TILE), jnp.float32))
        diagonals = jnp.concatenate(diagonals, axis=0)
    for half in range(plan.halves):
        for position in range(plan.positions):
            off = pl.multiple_of(plan.offset(half, position), 8)
            for at, (row, col) in enumerate(plan.sent):
                start = plan.start(position) + at * plan.rows
                outs[half][start : start + plan.rows, :] = acc[
                    pl.ds(row * TILE + off, plan.rows), col * TILE : (col + 1) * TILE
                ]
            if plan.folds:
                start = plan.start(position) + len(plan.sent) * plan.rows
                outs[half][start : start + plan.extra, :] = diagonals


def target_share(plan, t_ref, t_copy, flip, outs):
    head = lax.axis_index("head")
    core, y_at, plane = head % 2, (head // 2) % 2, head // 4
    strip = TILE // 4
    flip[...] = jnp.zeros_like(flip)
    t_copy.wait()
    flip[pl.ds(pl.multiple_of(strip * (2 * y_at + core), 8), strip), :] = t_ref[...].astype(jnp.float32)
    natural = pl.multiple_of(plan.offset(0, 0), 8)
    for col in range(plan.blocks):
        gap = (col - plane + plan.blocks) % plan.blocks
        is_natural = (2 * gap < plan.blocks) | ((2 * gap == plan.blocks) & (plane < col))
        keep_natural = jnp.where(is_natural, 1.0, 0.0)
        keep_flipped = jnp.where(is_natural & (gap != 0), 0.0, 1.0)
        cols = slice(col * TILE, (col + 1) * TILE)
        straight = flip[pl.ds(natural, plan.rows), cols] * keep_natural
        turned = (flip[:, cols] * keep_flipped).T
        flip[:, cols] = turned
        for half in range(plan.halves):
            off = pl.multiple_of(plan.offset(half, 0), 8)
            start = plan.size + col * plan.rows
            value = flip[pl.ds(off, plan.rows), cols]
            outs[half][start : start + plan.rows, :] = value + straight if half == 0 else value
            if col % 2 == 0:
                continue
            off = pl.multiple_of(plan.offset(half, 1), 8)
            start = plan.start(1) + plan.size + col // 2 * plan.rows
            before = flip[pl.ds(off, plan.rows), (col - 1) * TILE : col * TILE]
            outs[half][start : start + plan.rows, :] = before + pltpu.roll(
                flip[pl.ds(off, plan.rows), cols], TILE // 2, 1
            )


def probs_kernel(q_hbm, k_hbm, error_ref, p_ref, own_ref, q_ref, k_ref, qsem, ksem):
    count, length = q_ref.shape[0], q_ref.shape[1]
    group = group_of(count)
    q_copy = lambda step: pltpu.make_async_copy(
        q_hbm.at[pl.ds(step * group, group)], q_ref.at[pl.ds(step * group, group)], qsem.at[step]
    )
    k_copy = lambda step: pltpu.make_async_copy(
        k_hbm.at[pl.ds(step * group, group)], k_ref.at[pl.ds(step * group, group)], ksem.at[step]
    )
    for step in range(count // group):
        q_copy(step).start()
        k_copy(step).start()
    own_ref[...] = error_ref[...]


    def several(step, carry):
        q_copy(step).wait()
        k_copy(step).wait()
        for i in range(group):
            pair = step * group + i
            key = k_ref[pair]
            for part in range(length // FCHUNK):
                rows = slice(part * FCHUNK, (part + 1) * FCHUNK)
                p_ref[pair, rows, :] = softmax_rows(q_ref[pair, rows, :], key)
        return carry

    lax.fori_loop(0, count // group, several, 0)


def backward_kernel(plan, dims, hw_hbm, head_hbm, p_ref, q_ref, k_ref, rsum_ref, *rest):
    layer_count, slot_count, heads = dims
    count = layer_count * slot_count
    pieces = plan.halves * plan.positions
    packed = rest[:pieces]
    qg_hbm, kg_hbm, wg_ref, hw_ref, head_ref, fmat, shift_ref, qg_ref, kg_ref, sems, qsem, ksem = rest[pieces:]
    length = q_ref.shape[1]
    scale = q_ref.shape[2] ** (-0.5)
    total = 2.0 * length
    q_copy = lambda pair: pltpu.make_async_copy(qg_ref.at[pair], qg_hbm.at[pair], qsem.at[pair])
    k_copy = lambda pair: pltpu.make_async_copy(kg_ref.at[pair], kg_hbm.at[pair], ksem.at[pair])
    head_copy = fetch(head_hbm, head_ref, sems.at[1])
    hw_copy = fetch(hw_hbm, hw_ref, sems.at[0])
    lanes = lax.broadcasted_iota(jnp.int32, (plan.extra, TILE), 1) if plan.folds else None
    diagonals = 0.0
    for half in range(plan.halves):
        for position in range(plan.positions):
            off = pl.multiple_of(plan.offset(half, position), 8)
            if plan.folds:
                ends = packed[half * plan.positions + position][len(plan.sent) * plan.rows : plan.size, :]
                diagonals = diagonals + jnp.where((lanes >= off) & (lanes < off + plan.rows), ends, 0.0)
            for at, (row, col) in enumerate(plan.sent):
                fmat[pl.ds(row * TILE + off, plan.rows), col * TILE : (col + 1) * TILE] = packed[
                    half * plan.positions + position
                ][at * plan.rows : (at + 1) * plan.rows, :]
    if plan.folds:
        upper, middle = triangle()
        for at, (high, low) in enumerate(plan.folds):
            hs, ls = slice(high * TILE, (high + 1) * TILE), slice(low * TILE, (low + 1) * TILE)
            both = fmat[hs, hs]
            turned = both.T
            fmat[hs, hs] = jnp.where(upper, both, turned)
            fmat[ls, ls] = jnp.where(middle, diagonals[at : at + 1, :], jnp.where(upper, turned, both))
    for row, col in plan.pairs:
        if row != col:
            rs, cs = slice(row * TILE, (row + 1) * TILE), slice(col * TILE, (col + 1) * TILE)
            fmat[cs, rs] = fmat[rs, cs].T
    shifts = jnp.dot(
        rsum_ref[...], fmat[...], precision=lax.Precision.HIGHEST, preferred_element_type=jnp.float32
    ) * (1.0 / total)
    shift_ref[...] = shifts
    head_copy.wait()
    hw_copy.wait()

    group = group_of(count)

    def several(step, carry):
        pairs = [step * group + i for i in range(group)]
        for i, pair in enumerate(pairs):
            weight = pair_weight(hw_ref, head_ref, pair, slot_count, heads)
            shift = shift_ref[pl.ds(pair, 1), :]
            rowsum = rsum_ref[pl.ds(pair, 1), :]
            tops = jnp.zeros((8, 1), jnp.float32)
            parts = []
            for part in range(length // BCHUNK):
                rows = slice(part * BCHUNK, (part + 1) * BCHUNK)
                probs = p_ref[pair, rows, :]
                raised = probs * (fmat[rows, :] - shift)
                rowtotal = jnp.sum(raised, axis=1, keepdims=True)
                tops = tops + jnp.sum(rowtotal.reshape(BCHUNK // 8, 8, 1), axis=0)
                parts.append((weight * (raised - probs * rowtotal)).astype(jnp.bfloat16))
            dscores = jnp.concatenate(parts, axis=0)
            qgrad = jnp.dot(dscores, k_ref[pair], preferred_element_type=jnp.float32)
            qg_ref[pair] = (qgrad * scale).astype(jnp.bfloat16)
            kgrad = lax.dot_general(
                q_ref[pair], dscores, (((0,), (0,)), ((), ())), preferred_element_type=jnp.float32
            )
            kg_ref[pair] = (kgrad.T * scale).astype(jnp.bfloat16)
            grand = jnp.sum(shift * (0.5 * rowsum - 1.0), axis=1, keepdims=True) + jnp.sum(
                tops, axis=0, keepdims=True
            )
            wg_ref[pair // slot_count, pair % slot_count] = grand[0, 0]
            q_copy(pair).start()
            k_copy(pair).start()
        return carry

    lax.fori_loop(0, count // group, several, 0)
    for pair in range(count):
        q_copy(pair).wait()
        k_copy(pair).wait()


def swap(value, axis, size, flip):
    return lax.ppermute(value, axis, [(i, i ^ flip) for i in range(size)])


def across(value, layers, heads, layer_flip, head_flip):
    if layer_flip == 0:
        return swap(value, "head", heads, head_flip)
    if head_flip == 0:
        return swap(value, "layer", layers, layer_flip)
    pairs = [
        (la * heads + he, (la ^ layer_flip) * heads + (he ^ head_flip)) for la in range(layers) for he in range(heads)
    ]
    return lax.ppermute(value, ("layer", "head"), pairs)


def exchange_fast(plan, packed, probs_of):
    layers, heads, rows, blocks, size, share = plan.layers, plan.heads, plan.rows, plan.blocks, plan.size, plan.share
    chip = packed[0] + swap(packed[1], "head", heads, 1)
    got = []
    for position in range(1, plan.positions):
        value = chip[plan.start(position) : plan.start(position + 1)]
        got.append(across(value, layers, heads, position // 2, 2 * (position % 2)))
    y_at = (lax.axis_index("head") // 2) % 2
    theirs = lax.broadcasted_iota(jnp.int32, (share // 2, TILE), 1) // (TILE // 2) != y_at
    came = got[0][size:]
    evens = jnp.where(theirs, came, 0.0)
    odds = jnp.where(theirs, jnp.concatenate([came[:, TILE // 2 :], came[:, : TILE // 2]], axis=1), 0.0)
    parts = [half[at * rows : (at + 1) * rows] for at in range(blocks // 2) for half in (evens, odds)]
    tsym = chip[size : size + share] + jnp.concatenate(parts, axis=0)
    total = chip[:size]
    for value in got:
        total = total + value[:size]
    planes = {0: tsym}
    flip = blocks // 2
    while flip:
        order = sorted(planes)
        came = swap(jnp.concatenate([total] + [planes[i] for i in order], axis=0), "head", heads, 4 * flip)
        total = total + came[:size]
        for at, i in enumerate(order):
            planes[i ^ flip] = came[size + at * share : size + (at + 1) * share]
        flip = flip // 2
    plane = lax.axis_index("head") // 4

    def shared(row, col):
        value = planes[0]
        for flip in range(1, blocks):
            value = jnp.where((plane ^ flip) == row, planes[flip], value)
        return value[col * rows : (col + 1) * rows]

    off = plan.offset(0, 0)
    lows = dict(plan.folds)
    at_row = lax.broadcasted_iota(jnp.int32, (rows, TILE), 0) + off
    at_col = lax.broadcasted_iota(jnp.int32, (rows, TILE), 1)
    tparts = []
    for row, col in plan.sent:
        if row != col:
            tparts.append(shared(row, col) + shared(col, row))
        elif row in lows:
            tparts.append(jnp.where(at_col >= at_row, shared(row, row), shared(lows[row], lows[row])))
        else:
            tparts.append(shared(row, row))
    if plan.folds:
        ends = [jnp.sum(jnp.where(at_col == at_row, shared(low, low), 0.0), axis=0, keepdims=True) for _, low in plan.folds]
        tparts.append(jnp.pad(jnp.concatenate(ends, axis=0), ((0, plan.extra - len(ends)), (0, 0))))
    error = 2.0 * jax.nn.sigmoid(total) - jnp.concatenate(tparts, axis=0)
    parts = []
    for position in range(1, plan.positions):
        parts.append(across(error, layers, heads, position // 2, 2 * (position % 2)))
    probs, error, *vectors = probs_of(error)
    mine = [error] + parts
    return [probs] + vectors, mine + [swap(part, "head", heads, 1) for part in mine]


def exchange_general(plan, packed, target, probs_of):
    logit = lax.psum(packed[0], ("layer", "head"))
    whole = lax.all_gather(target, "head", axis=0, tiled=True)
    whole = (whole + whole.T).astype(jnp.float32)
    parts = [whole[r * TILE : (r + 1) * TILE, c * TILE : (c + 1) * TILE] for r, c in plan.pairs]
    probs, error, *vectors = probs_of(2.0 * jax.nn.sigmoid(logit) - jnp.concatenate(parts, axis=0))
    return [probs] + vectors, [error]


def on_device(layers, heads_axis, queries, keys, head_weight, slot_head, target):
    layer_count, slot_count, length, size = queries.shape
    heads = head_weight.shape[1]
    count = layer_count * slot_count
    plan = Plan(layers, heads_axis, length)
    flat_q = queries.reshape(count, length, size)
    flat_k = keys.reshape(count, length, size)
    dims = (layer_count, slot_count, heads)
    hbm = pl.BlockSpec(memory_space=pltpu.HBM)
    vmem = pl.BlockSpec(memory_space=pltpu.VMEM)
    smem = pl.BlockSpec(memory_space=pltpu.SMEM)
    sums_shape = (pad8(count), length)
    params = pltpu.CompilerParams(vmem_limit_bytes=32 * 2**20)
    weights = [pltpu.SMEM(head_weight.shape, jnp.float32), pltpu.SMEM(slot_head.shape, jnp.int32)]
    pair_sems = pltpu.SemaphoreType.DMA((count,))
    head_weight, target_hbm, first_q, first_k = (
        pltpu.with_memory_space_constraint(value, pltpu.HBM) for value in (head_weight, target, flat_q, flat_k)
    )
    if slot_count > 1:
        slot_head = pltpu.with_memory_space_constraint(slot_head, pltpu.HBM)
    fwd = pl.pallas_call(
        functools.partial(forward_kernel, plan, dims),
        in_specs=[hbm] * 5,
        out_specs=[vmem] * (plan.halves + 1),
        out_shape=[pltpu.VMEM((plan.start(plan.positions), TILE), jnp.float32)] * plan.halves
        + [pltpu.VMEM(sums_shape, jnp.float32)],
        scratch_shapes=weights
        + [
            pltpu.VMEM(target.shape, jnp.int32),
            pltpu.VMEM(flat_q.shape, jnp.bfloat16),
            pltpu.VMEM(flat_q.shape, jnp.bfloat16),
            pltpu.VMEM((length, length), jnp.float32),
            pltpu.VMEM(sums_shape, jnp.float32),
            pltpu.VMEM((TILE, length), jnp.float32),
            pltpu.SemaphoreType.DMA((3,)),
            pair_sems,
            pair_sems,
        ],
        compiler_params=params,
        name="forward_maps",
    )(head_weight, slot_head, target_hbm, first_q, first_k)
    packed, rsum = fwd[: plan.halves], fwd[plan.halves]

    def probs_of(error):
        return pl.pallas_call(
            probs_kernel,
            in_specs=[hbm, hbm, vmem],
            out_specs=[vmem] * 4,
            out_shape=[
                pltpu.VMEM((count, length, length), jnp.float32),
                pltpu.VMEM(error.shape, jnp.float32),
                pltpu.VMEM(flat_q.shape, jnp.bfloat16),
                pltpu.VMEM(flat_q.shape, jnp.bfloat16),
            ],
            scratch_shapes=[pair_sems, pair_sems],
            compiler_params=params,
            cost_estimate=pl.CostEstimate(
                flops=2 * count * length * length * size,
                bytes_accessed=4 * count * length * length,
                transcendentals=count * length * length,
            ),
            name="probs_maps",
        )(first_q, first_k, error)

    if plan.fast:
        held, errors = exchange_fast(plan, packed, probs_of)
    else:
        held, errors = exchange_general(plan, packed, target, probs_of)
    qgrad, kgrad, wgrad = pl.pallas_call(
        functools.partial(backward_kernel, plan, dims),
        in_specs=[hbm] * 2 + [vmem] * (4 + plan.halves * plan.positions),
        out_specs=[hbm, hbm, smem],
        out_shape=[
            pltpu.HBM((count, length, size), jnp.bfloat16),
            pltpu.HBM((count, length, size), jnp.bfloat16),
            jax.ShapeDtypeStruct((layer_count, slot_count), jnp.float32),
        ],
        scratch_shapes=weights
        + [
            pltpu.VMEM((length, length), jnp.float32),
            pltpu.VMEM(sums_shape, jnp.float32),
            pltpu.VMEM(flat_q.shape, jnp.bfloat16),
            pltpu.VMEM(flat_q.shape, jnp.bfloat16),
            pltpu.SemaphoreType.DMA((2,)),
            pair_sems,
            pair_sems,
        ],
        compiler_params=params,
        name="backward_maps",
    )(head_weight, slot_head, *held, rsum, *errors)
    return qgrad.reshape(queries.shape), kgrad.reshape(queries.shape), wgrad


def solution(mesh):
    return jax.shard_map(
        functools.partial(on_device, mesh.shape["layer"], mesh.shape["head"]),
        mesh=mesh,
        in_specs=(
            P("layer", "head", None, None),
            P("layer", "head", None, None),
            P("layer", None),
            P("head"),
            P("head", None),
        ),
        out_specs=(
            P("layer", "head", None, None),
            P("layer", "head", None, None),
            P("layer", "head"),
        ),
        check_vma=False,
    )
```

```python
import functools

import jax
import jax.numpy as jnp
from jax import lax
from jax.experimental import pallas as pl
from jax.experimental.pallas import tpu as pltpu
from jax.sharding import PartitionSpec as P

TILE = 128
LOG2E = 1.4426950408889634
FCHUNK = 256
BCHUNK = 256


def block_pairs(count):
    pairs = []
    for row in range(count):
        for col in range(count):
            gap = (col - row) % count
            if 2 * gap < count or (2 * gap == count and row < col):
                pairs.append((row, col))
    return pairs


def group_of(count):
    return 3 if count % 3 == 0 else 2 if count % 2 == 0 else 1


def pad8(count):
    return -(-count // 8) * 8


def split3(value):
    first = value.astype(jnp.bfloat16).astype(jnp.float32)
    rest = value - first
    second = rest.astype(jnp.bfloat16).astype(jnp.float32)
    return first, second, rest - second


def pair_weight(hw_ref, head_ref, pair, slot_count, heads):
    layer, slot = pair // slot_count, pair % slot_count
    held = head_ref[slot]
    return jnp.where(held < heads, hw_ref[layer, jnp.minimum(held, heads - 1)], 0.0)


class Plan:
    def __init__(self, layers, heads, length):
        self.blocks = length // TILE
        self.pairs = block_pairs(self.blocks)
        self.layers, self.heads = layers, heads
        self.fast = (
            heads % 4 == 0
            and heads // 4 == self.blocks
            and self.blocks & (self.blocks - 1) == 0
            and layers & (layers - 1) == 0
            and (TILE // (4 * layers)) % 8 == 0
        )
        self.halves = 2 if self.fast else 1
        self.positions = 2 * layers if self.fast else 1
        self.rows = TILE // (self.halves * self.positions)
        self.folds = [(i, i + 1) for i in range(0, self.blocks, 2)] if self.fast and self.blocks % 2 == 0 else []
        lower = [low for _, low in self.folds]
        self.sent = [(row, col) for row, col in self.pairs if row != col or row not in lower]
        self.extra = pad8(len(self.folds))
        self.size = len(self.sent) * self.rows + self.extra
        self.share = self.blocks * self.rows if self.fast else 0

    def start(self, position):
        return position * self.size + min(position, 1) * self.share + (self.share // 2 if position > 1 else 0)

    def offset(self, half, position):
        if not self.fast:
            return 0
        head = lax.axis_index("head")
        core = (head % 2) ^ half
        y_at = ((head // 2) % 2) ^ (position % 2)
        layer = lax.axis_index("layer") ^ (position // 2)
        return ((2 * y_at + core) * self.layers + layer) * self.rows


def triangle():
    rows = lax.broadcasted_iota(jnp.int32, (TILE, TILE), 0)
    cols = lax.broadcasted_iota(jnp.int32, (TILE, TILE), 1)
    return cols >= rows, cols == rows


def fetch(source, target, sem):
    copy = pltpu.make_async_copy(source, target, sem)
    copy.start()
    return copy


def softmax_rows(query, key):
    scores = lax.dot_general(query, key, (((1,), (1,)), ((), ())), preferred_element_type=jnp.float32)
    highest = jnp.max(scores, axis=1, keepdims=True)
    expo = jnp.exp2((scores - highest) * (LOG2E * query.shape[-1] ** (-0.5)))
    return expo * (1.0 / jnp.sum(expo, axis=1, keepdims=True))


def forward_kernel(plan, dims, hw_hbm, head_hbm, t_hbm, q_hbm, k_hbm, *rest):
    layer_count, slot_count, heads = dims
    count = layer_count * slot_count
    outs, rsum_ref = rest[: plan.halves], rest[plan.halves]
    hw_ref, head_ref, t_ref, q_ref, k_ref, acc, scaled, flip, sems, qsem, ksem = rest[plan.halves + 1 :]
    length = q_ref.shape[1]
    total = 2.0 * length
    group = group_of(count)
    q_copy = lambda step: pltpu.make_async_copy(
        q_hbm.at[pl.ds(step * group, group)], q_ref.at[pl.ds(step * group, group)], qsem.at[step]
    )
    k_copy = lambda step: pltpu.make_async_copy(
        k_hbm.at[pl.ds(step * group, group)], k_ref.at[pl.ds(step * group, group)], ksem.at[step]
    )
    t_copy = fetch(t_hbm, t_ref, sems.at[2])
    for step in range(count // group):
        q_copy(step).start()
        k_copy(step).start()
        if step == 0:
            head_copy = fetch(head_hbm, head_ref, sems.at[1])
            hw_copy = fetch(hw_hbm, hw_ref, sems.at[0])
    acc[...] = jnp.zeros_like(acc)
    scaled[...] = jnp.zeros_like(scaled)
    rsum_ref[...] = jnp.zeros_like(rsum_ref)
    if plan.fast:
        target_share(plan, t_ref, t_copy, flip, outs)
    else:
        t_copy.wait()
    head_copy.wait()
    hw_copy.wait()

    def several(step, carry):
        pairs = [step * group + i for i in range(group)]
        q_copy(step).wait()
        k_copy(step).wait()
        weights = [pair_weight(hw_ref, head_ref, pair, slot_count, heads) for pair in pairs]
        colsums = [jnp.zeros((8, length), jnp.float32) for _ in pairs]
        for part in range(length // FCHUNK):
            rows = slice(part * FCHUNK, (part + 1) * FCHUNK)
            added = acc[rows, :]
            for i, pair in enumerate(pairs):
                probs = softmax_rows(q_ref[pair, rows, :], k_ref[pair])
                added = added + weights[i] * probs
                colsums[i] = colsums[i] + jnp.sum(probs.reshape(FCHUNK // 8, 8, length), axis=0)
            acc[rows, :] = added
        for i, pair in enumerate(pairs):
            rowsum = 1.0 + jnp.sum(colsums[i], axis=0, keepdims=True)
            rsum_ref[pl.ds(pair, 1), :] = rowsum
            scaled[pl.ds(pair, 1), :] = rowsum * (-weights[i] / total)
        return carry

    lax.fori_loop(0, count // group, several, 0)
    left = split3(scaled[...])
    right = split3(rsum_ref[...])
    order = ((0, 0), (0, 1), (1, 0), (1, 1), (0, 2), (2, 0))
    lefts = jnp.concatenate([left[a] for a, _ in order], axis=0).astype(jnp.bfloat16)
    rights = jnp.concatenate([right[b] for _, b in order], axis=0).astype(jnp.bfloat16)
    for row, col in plan.pairs:
        rs, cs = slice(row * TILE, (row + 1) * TILE), slice(col * TILE, (col + 1) * TILE)
        both = acc[rs, cs] + acc[cs, rs].T
        acc[rs, cs] = both + lax.dot_general(
            lefts[:, rs], rights[:, cs], (((0,), (0,)), ((), ())), preferred_element_type=jnp.float32
        )
    diagonals = []
    if plan.folds:
        upper, middle = triangle()
        for high, low in plan.folds:
            hs, ls = slice(high * TILE, (high + 1) * TILE), slice(low * TILE, (low + 1) * TILE)
            below = acc[ls, ls]
            acc[hs, hs] = jnp.where(upper, acc[hs, hs], below)
            diagonals.append(jnp.sum(jnp.where(middle, below, 0.0), axis=0, keepdims=True))
        diagonals.append(jnp.zeros((plan.extra - len(plan.folds), TILE), jnp.float32))
        diagonals = jnp.concatenate(diagonals, axis=0)
    for half in range(plan.halves):
        for position in range(plan.positions):
            off = pl.multiple_of(plan.offset(half, position), 8)
            for at, (row, col) in enumerate(plan.sent):
                start = plan.start(position) + at * plan.rows
                outs[half][start : start + plan.rows, :] = acc[
                    pl.ds(row * TILE + off, plan.rows), col * TILE : (col + 1) * TILE
                ]
            if plan.folds:
                start = plan.start(position) + len(plan.sent) * plan.rows
                outs[half][start : start + plan.extra, :] = diagonals


def target_share(plan, t_ref, t_copy, flip, outs):
    head = lax.axis_index("head")
    core, y_at, plane = head % 2, (head // 2) % 2, head // 4
    strip = TILE // 4
    flip[...] = jnp.zeros_like(flip)
    t_copy.wait()
    flip[pl.ds(pl.multiple_of(strip * (2 * y_at + core), 8), strip), :] = t_ref[...].astype(jnp.float32)
    natural = pl.multiple_of(plan.offset(0, 0), 8)
    for col in range(plan.blocks):
        gap = (col - plane + plan.blocks) % plan.blocks
        is_natural = (2 * gap < plan.blocks) | ((2 * gap == plan.blocks) & (plane < col))
        keep_natural = jnp.where(is_natural, 1.0, 0.0)
        keep_flipped = jnp.where(is_natural & (gap != 0), 0.0, 1.0)
        cols = slice(col * TILE, (col + 1) * TILE)
        straight = flip[pl.ds(natural, plan.rows), cols] * keep_natural
        turned = (flip[:, cols] * keep_flipped).T
        flip[:, cols] = turned
        for half in range(plan.halves):
            off = pl.multiple_of(plan.offset(half, 0), 8)
            start = plan.size + col * plan.rows
            value = flip[pl.ds(off, plan.rows), cols]
            outs[half][start : start + plan.rows, :] = value + straight if half == 0 else value
            if col % 2 == 0:
                continue
            off = pl.multiple_of(plan.offset(half, 1), 8)
            start = plan.start(1) + plan.size + col // 2 * plan.rows
            before = flip[pl.ds(off, plan.rows), (col - 1) * TILE : col * TILE]
            outs[half][start : start + plan.rows, :] = before + pltpu.roll(
                flip[pl.ds(off, plan.rows), cols], TILE // 2, 1
            )


def probs_kernel(q_hbm, k_hbm, error_ref, p_ref, own_ref, q_ref, k_ref, qsem, ksem):
    count, length = q_ref.shape[0], q_ref.shape[1]
    group = group_of(count)
    q_copy = lambda step: pltpu.make_async_copy(
        q_hbm.at[pl.ds(step * group, group)], q_ref.at[pl.ds(step * group, group)], qsem.at[step]
    )
    k_copy = lambda step: pltpu.make_async_copy(
        k_hbm.at[pl.ds(step * group, group)], k_ref.at[pl.ds(step * group, group)], ksem.at[step]
    )
    for step in range(count // group):
        q_copy(step).start()
        k_copy(step).start()
    own_ref[...] = error_ref[...]


    def several(step, carry):
        q_copy(step).wait()
        k_copy(step).wait()
        for i in range(group):
            pair = step * group + i
            key = k_ref[pair]
            for part in range(length // FCHUNK):
                rows = slice(part * FCHUNK, (part + 1) * FCHUNK)
                p_ref[pair, rows, :] = softmax_rows(q_ref[pair, rows, :], key)
        return carry

    lax.fori_loop(0, count // group, several, 0)


def backward_kernel(plan, dims, hw_hbm, head_hbm, p_ref, q_ref, k_ref, rsum_ref, *rest):
    layer_count, slot_count, heads = dims
    count = layer_count * slot_count
    pieces = plan.halves * plan.positions
    packed = rest[:pieces]
    qg_hbm, kg_hbm, wg_ref, hw_ref, head_ref, fmat, shift_ref, dmat, qg_ref, kg_ref, sems, qsem, ksem = rest[pieces:]
    length = q_ref.shape[1]
    scale = q_ref.shape[2] ** (-0.5)
    total = 2.0 * length
    q_copy = lambda pair: pltpu.make_async_copy(qg_ref.at[pair], qg_hbm.at[pair], qsem.at[pair])
    k_copy = lambda pair: pltpu.make_async_copy(kg_ref.at[pair], kg_hbm.at[pair], ksem.at[pair])
    head_copy = fetch(head_hbm, head_ref, sems.at[1])
    hw_copy = fetch(hw_hbm, hw_ref, sems.at[0])
    lanes = lax.broadcasted_iota(jnp.int32, (plan.extra, TILE), 1) if plan.folds else None
    diagonals = 0.0
    for half in range(plan.halves):
        for position in range(plan.positions):
            off = pl.multiple_of(plan.offset(half, position), 8)
            if plan.folds:
                ends = packed[half * plan.positions + position][len(plan.sent) * plan.rows : plan.size, :]
                diagonals = diagonals + jnp.where((lanes >= off) & (lanes < off + plan.rows), ends, 0.0)
            for at, (row, col) in enumerate(plan.sent):
                fmat[pl.ds(row * TILE + off, plan.rows), col * TILE : (col + 1) * TILE] = packed[
                    half * plan.positions + position
                ][at * plan.rows : (at + 1) * plan.rows, :]
    if plan.folds:
        upper, middle = triangle()
        for at, (high, low) in enumerate(plan.folds):
            hs, ls = slice(high * TILE, (high + 1) * TILE), slice(low * TILE, (low + 1) * TILE)
            both = fmat[hs, hs]
            turned = both.T
            fmat[hs, hs] = jnp.where(upper, both, turned)
            fmat[ls, ls] = jnp.where(middle, diagonals[at : at + 1, :], jnp.where(upper, turned, both))
    for row, col in plan.pairs:
        if row != col:
            rs, cs = slice(row * TILE, (row + 1) * TILE), slice(col * TILE, (col + 1) * TILE)
            fmat[cs, rs] = fmat[rs, cs].T
    shifts = jnp.dot(
        rsum_ref[...], fmat[...], precision=lax.Precision.HIGHEST, preferred_element_type=jnp.float32
    ) * (1.0 / total)
    shift_ref[...] = shifts
    head_copy.wait()
    hw_copy.wait()

    group = group_of(count)

    def several(step, carry):
        pairs = [step * group + i for i in range(group)]
        for i, pair in enumerate(pairs):
            weight = pair_weight(hw_ref, head_ref, pair, slot_count, heads)
            shift = shift_ref[pl.ds(pair, 1), :]
            rowsum = rsum_ref[pl.ds(pair, 1), :]
            tops = jnp.zeros((8, 1), jnp.float32)
            for part in range(length // BCHUNK):
                rows = slice(part * BCHUNK, (part + 1) * BCHUNK)
                probs = p_ref[pair, rows, :]
                raised = probs * (fmat[rows, :] - shift)
                rowtotal = jnp.sum(raised, axis=1, keepdims=True)
                tops = tops + jnp.sum(rowtotal.reshape(BCHUNK // 8, 8, 1), axis=0)
                dmat[i, rows, :] = (weight * (raised - probs * rowtotal)).astype(jnp.bfloat16)
            qgrad = jnp.dot(dmat[i], k_ref[pair], preferred_element_type=jnp.float32)
            qg_ref[pair] = (qgrad * scale).astype(jnp.bfloat16)
            kgrad = lax.dot_general(
                q_ref[pair], dmat[i], (((0,), (0,)), ((), ())), preferred_element_type=jnp.float32
            )
            kg_ref[pair] = (kgrad.T * scale).astype(jnp.bfloat16)
            grand = jnp.sum(shift * (0.5 * rowsum - 1.0), axis=1, keepdims=True) + jnp.sum(
                tops, axis=0, keepdims=True
            )
            wg_ref[pair // slot_count, pair % slot_count] = grand[0, 0]
            q_copy(pair).start()
            k_copy(pair).start()
        return carry

    lax.fori_loop(0, count // group, several, 0)
    for pair in range(count):
        q_copy(pair).wait()
        k_copy(pair).wait()


def swap(value, axis, size, flip):
    return lax.ppermute(value, axis, [(i, i ^ flip) for i in range(size)])


def across(value, layers, heads, layer_flip, head_flip):
    if layer_flip == 0:
        return swap(value, "head", heads, head_flip)
    if head_flip == 0:
        return swap(value, "layer", layers, layer_flip)
    pairs = [
        (la * heads + he, (la ^ layer_flip) * heads + (he ^ head_flip)) for la in range(layers) for he in range(heads)
    ]
    return lax.ppermute(value, ("layer", "head"), pairs)


def exchange_fast(plan, packed, probs_of):
    layers, heads, rows, blocks, size, share = plan.layers, plan.heads, plan.rows, plan.blocks, plan.size, plan.share
    chip = packed[0] + swap(packed[1], "head", heads, 1)
    got = []
    for position in range(1, plan.positions):
        value = chip[plan.start(position) : plan.start(position + 1)]
        got.append(across(value, layers, heads, position // 2, 2 * (position % 2)))
    y_at = (lax.axis_index("head") // 2) % 2
    theirs = lax.broadcasted_iota(jnp.int32, (share // 2, TILE), 1) // (TILE // 2) != y_at
    came = got[0][size:]
    evens = jnp.where(theirs, came, 0.0)
    odds = jnp.where(theirs, jnp.concatenate([came[:, TILE // 2 :], came[:, : TILE // 2]], axis=1), 0.0)
    parts = [half[at * rows : (at + 1) * rows] for at in range(blocks // 2) for half in (evens, odds)]
    tsym = chip[size : size + share] + jnp.concatenate(parts, axis=0)
    total = chip[:size]
    for value in got:
        total = total + value[:size]
    plane = lax.axis_index("head") // 4
    off = plan.offset(0, 0)
    lows = dict(plan.folds)
    at_row = lax.broadcasted_iota(jnp.int32, (rows, TILE), 0) + off
    at_col = lax.broadcasted_iota(jnp.int32, (rows, TILE), 1)

    def packed_share(known):
        def shared(row, col):
            value = jnp.zeros((rows, TILE), jnp.float32)
            for flip, share_of in known.items():
                value = jnp.where((plane ^ flip) == row, share_of[col * rows : (col + 1) * rows], value)
            return value

        tparts = []
        for row, col in plan.sent:
            if row != col:
                tparts.append(shared(row, col) + shared(col, row))
            elif row in lows:
                tparts.append(jnp.where(at_col >= at_row, shared(row, row), shared(lows[row], lows[row])))
            else:
                tparts.append(shared(row, row))
        if plan.folds:
            ends = [
                jnp.sum(jnp.where(at_col == at_row, shared(low, low), 0.0), axis=0, keepdims=True)
                for _, low in plan.folds
            ]
            tparts.append(jnp.pad(jnp.concatenate(ends, axis=0), ((0, plan.extra - len(ends)), (0, 0))))
        return jnp.concatenate(tparts, axis=0)

    planes = {0: tsym}
    early, late = 0.0, planes
    flip = blocks // 2
    while flip:
        order = sorted(planes)
        came = swap(jnp.concatenate([total] + [planes[i] for i in order], axis=0), "head", heads, 4 * flip)
        total = total + came[:size]
        late = {i ^ flip: came[size + at * share : size + (at + 1) * share] for at, i in enumerate(order)}
        early = packed_share(planes)
        planes = planes | late
        flip = flip // 2
    error = (2.0 * jax.nn.sigmoid(total) - early) - packed_share(late)
    parts = []
    for position in range(1, plan.positions):
        parts.append(across(error, layers, heads, position // 2, 2 * (position % 2)))
    probs, error, *vectors = probs_of(error)
    mine = [error] + parts
    return [probs] + vectors, mine + [swap(part, "head", heads, 1) for part in mine]


def exchange_general(plan, packed, target, probs_of):
    logit = lax.psum(packed[0], ("layer", "head"))
    whole = lax.all_gather(target, "head", axis=0, tiled=True)
    whole = (whole + whole.T).astype(jnp.float32)
    parts = [whole[r * TILE : (r + 1) * TILE, c * TILE : (c + 1) * TILE] for r, c in plan.pairs]
    probs, error, *vectors = probs_of(2.0 * jax.nn.sigmoid(logit) - jnp.concatenate(parts, axis=0))
    return [probs] + vectors, [error]


def on_device(layers, heads_axis, queries, keys, head_weight, slot_head, target):
    layer_count, slot_count, length, size = queries.shape
    heads = head_weight.shape[1]
    count = layer_count * slot_count
    plan = Plan(layers, heads_axis, length)
    flat_q = queries.reshape(count, length, size)
    flat_k = keys.reshape(count, length, size)
    dims = (layer_count, slot_count, heads)
    hbm = pl.BlockSpec(memory_space=pltpu.HBM)
    vmem = pl.BlockSpec(memory_space=pltpu.VMEM)
    smem = pl.BlockSpec(memory_space=pltpu.SMEM)
    sums_shape = (pad8(count), length)
    params = pltpu.CompilerParams(vmem_limit_bytes=12 * 2**20)
    weights = [pltpu.SMEM(head_weight.shape, jnp.float32), pltpu.SMEM(slot_head.shape, jnp.int32)]
    pair_sems = pltpu.SemaphoreType.DMA((count,))
    head_weight, target_hbm, first_q, first_k = (
        pltpu.with_memory_space_constraint(value, pltpu.HBM) for value in (head_weight, target, flat_q, flat_k)
    )
    if slot_count > 1:
        slot_head = pltpu.with_memory_space_constraint(slot_head, pltpu.HBM)
    fwd = pl.pallas_call(
        functools.partial(forward_kernel, plan, dims),
        in_specs=[hbm] * 5,
        out_specs=[vmem] * (plan.halves + 1),
        out_shape=[pltpu.VMEM((plan.start(plan.positions), TILE), jnp.float32)] * plan.halves
        + [pltpu.VMEM(sums_shape, jnp.float32)],
        scratch_shapes=weights
        + [
            pltpu.VMEM(target.shape, jnp.int32),
            pltpu.VMEM(flat_q.shape, jnp.bfloat16),
            pltpu.VMEM(flat_q.shape, jnp.bfloat16),
            pltpu.VMEM((length, length), jnp.float32),
            pltpu.VMEM(sums_shape, jnp.float32),
            pltpu.VMEM((TILE, length), jnp.float32),
            pltpu.SemaphoreType.DMA((3,)),
            pair_sems,
            pair_sems,
        ],
        compiler_params=params,
        name="forward_maps",
    )(head_weight, slot_head, target_hbm, first_q, first_k)
    packed, rsum = fwd[: plan.halves], fwd[plan.halves]

    def probs_of(error):
        return pl.pallas_call(
            probs_kernel,
            in_specs=[hbm, hbm, vmem],
            out_specs=[vmem] * 4,
            out_shape=[
                pltpu.VMEM((count, length, length), jnp.float32),
                pltpu.VMEM(error.shape, jnp.float32),
                pltpu.VMEM(flat_q.shape, jnp.bfloat16),
                pltpu.VMEM(flat_q.shape, jnp.bfloat16),
            ],
            scratch_shapes=[pair_sems, pair_sems],
            compiler_params=params,
            cost_estimate=pl.CostEstimate(
                flops=2 * count * length * length * size,
                bytes_accessed=4 * count * length * length,
                transcendentals=count * length * length,
            ),
            name="probs_maps",
        )(first_q, first_k, error)

    if plan.fast:
        held, errors = exchange_fast(plan, packed, probs_of)
    else:
        held, errors = exchange_general(plan, packed, target, probs_of)
    qgrad, kgrad, wgrad = pl.pallas_call(
        functools.partial(backward_kernel, plan, dims),
        in_specs=[hbm] * 2 + [vmem] * (4 + plan.halves * plan.positions),
        out_specs=[hbm, hbm, smem],
        out_shape=[
            pltpu.HBM((count, length, size), jnp.bfloat16),
            pltpu.HBM((count, length, size), jnp.bfloat16),
            jax.ShapeDtypeStruct((layer_count, slot_count), jnp.float32),
        ],
        scratch_shapes=weights
        + [
            pltpu.VMEM((length, length), jnp.float32),
            pltpu.VMEM(sums_shape, jnp.float32),
            pltpu.VMEM((group_of(count), length, length), jnp.bfloat16),
            pltpu.VMEM(flat_q.shape, jnp.bfloat16),
            pltpu.VMEM(flat_q.shape, jnp.bfloat16),
            pltpu.SemaphoreType.DMA((2,)),
            pair_sems,
            pair_sems,
        ],
        compiler_params=params,
        name="backward_maps",
    )(head_weight, slot_head, *held, rsum, *errors)
    return qgrad.reshape(queries.shape), kgrad.reshape(queries.shape), wgrad


def solution(mesh):
    return jax.shard_map(
        functools.partial(on_device, mesh.shape["layer"], mesh.shape["head"]),
        mesh=mesh,
        in_specs=(
            P("layer", "head", None, None),
            P("layer", "head", None, None),
            P("layer", None),
            P("head"),
            P("head", None),
        ),
        out_specs=(
            P("layer", "head", None, None),
            P("layer", "head", None, None),
            P("layer", "head"),
        ),
        check_vma=False,
    )
```
